32 devices in a mesh: flat: 32 (over z, y, x, core).
Axes of the slice: x: 2, y: 2, z: 4, core: 2. Of those that a mesh axis runs over, the one named last changes fastest.
Arguments:
- hidden_in: bfloat16 [32768, 640], P('flat'), may hold values from -6 to 6
- segments: int32 [32768], P('flat'), may hold values from 0 to 32, as said below
- w_query: bfloat16 [655360], P('flat'), may hold values from -0.25 to 0.25
- w_key: bfloat16 [163840], P('flat'), may hold values from -0.25 to 0.25
- w_value: bfloat16 [163840], P('flat'), may hold values from -0.25 to 0.25
- w_out: bfloat16 [655360], P('flat'), may hold values from -0.1875 to 0.1875
- w_gate: bfloat16 [1310720], P('flat'), may hold values from -0.25 to 0.25
- w_up: bfloat16 [1310720], P('flat'), may hold values from -0.25 to 0.25
- w_down: bfloat16 [1310720], P('flat'), may hold values from -0.125 to 0.125
- norm_gains: bfloat16 [3072], P('flat'), may hold values from 0.5 to 1.5
- cotangent: bfloat16 [32768, 640], P('flat'), may hold values from -6 to 6
Outputs:
- output: bfloat16 [32768, 640], P('flat')
- grad_in: bfloat16 [32768, 640], P('flat')
- grad_query: float32 [655360], P('flat')
- grad_key: float32 [163840], P('flat')
- grad_value: float32 [163840], P('flat')
- grad_out: float32 [655360], P('flat')
- grad_gate: float32 [1310720], P('flat')
- grad_up: float32 [1310720], P('flat')
- grad_down: float32 [1310720], P('flat')
- grad_gains: float32 [3072], P('flat')
The draws below stay inside these ranges and needn't reach their ends.
Inputs may be any that keep to these rules, and one draw needn't show every extreme that they name: `segments`: segment numbers never fall; the first token has number 0; each block of 1024 tokens of one device holds exactly one position other than its first at which the number rises, by one.
All inputs are finite; a program needn't handle non-finite values.
Results may differ from the reference program's by a relative error of at most 0.017.
Values may be sent and summed in bfloat16 or wider, within the bound.
No kernel may reach another device: no remote copies, remote signals or barrier semaphores. Data moves between devices by JAX's collectives and lax.ppermute only.
A program may use at most 192 MiB of HBM per device.

```python
import jax
import jax.numpy as jnp
from jax import lax

D = 640
NH = 4
HD = 256
FF = 2048
WINDOW = 512
TOK_DEV = 1024
TOKENS = 32768
GAIN_LEN = 3072


def draw_segments(key, part):
    key = jax.random.fold_in(key, 11)
    blocks = TOKENS // TOK_DEV
    borders = jax.random.randint(key, (blocks,), 1, TOK_DEV, dtype=jnp.int32)
    index = jnp.arange(TOKENS, dtype=jnp.int32)
    owner = index // TOK_DEV
    within = index - owner * TOK_DEV
    return (owner + (within >= jnp.take(borders, owner)).astype(jnp.int32)).astype(jnp.int32)


def levels(stream_key, dims, split, low, high):
    def one(axis_at, parts):
        draws = jax.random.uniform(jax.random.fold_in(jax.random.fold_in(stream_key, 6), axis_at), (parts,), jnp.float32, low / len(split), high / len(split))
        return jnp.repeat(jnp.exp(draws), dims[axis_at] // parts).reshape((-1,) + (1,) * (len(dims) - axis_at - 1))

    level = one(*split[0])
    for cut in split[1:]:
        level = level * one(*cut)
    return level


def centred(key, dims, width, reach, cuts=(), held_as=jnp.bfloat16):
    loudness = levels(key, dims, cuts, -0.22, 0.18) if cuts else 1.0
    drawn = jax.random.normal(key, dims, jnp.float32) * width * loudness
    return jnp.minimum(jnp.maximum(drawn, -reach), reach).astype(held_as)


def setup_inputs(seed: int = 0) -> dict:
    keys = jax.random.split(jax.random.key(seed), 12)
    hidden_in = centred(keys[0], (TOKENS, D), 1.0, 6.0, ((0, 32),))
    segments = draw_segments(jax.random.fold_in(keys[11], 71), 0)
    w_query = centred(keys[2], (D * NH * HD,), D ** -0.5, 0.25, ((0, 32),))
    w_key = centred(keys[3], (D * HD,), D ** -0.5, 0.25, ((0, 32),))
    w_value = centred(keys[4], (D * HD,), D ** -0.5, 0.25, ((0, 32),))
    w_out = centred(keys[5], (NH * HD * D,), (NH * HD) ** -0.5, 0.1875, ((0, 32),))
    w_gate = centred(keys[6], (D * FF,), D ** -0.5, 0.25, ((0, 32),))
    w_up = centred(keys[7], (D * FF,), D ** -0.5, 0.25, ((0, 32),))
    w_down = centred(keys[8], (FF * D,), FF ** -0.5, 0.125, ((0, 32),))
    norm_gains = jnp.clip(1.0 + 0.1 * jax.random.normal(keys[9], (GAIN_LEN,), jnp.float32), 0.5, 1.5).astype(jnp.bfloat16)
    cotangent = centred(keys[10], (TOKENS, D), 1.0, 6.0, ((0, 32),))
    return dict(hidden_in=hidden_in, segments=segments, w_query=w_query, w_key=w_key, w_value=w_value, w_out=w_out, w_gate=w_gate, w_up=w_up, w_down=w_down, norm_gains=norm_gains, cotangent=cotangent)


@jax.custom_vjp
def low(v):
    return lax.optimization_barrier(v.astype(jnp.bfloat16)).astype(jnp.float32)

@jax.custom_vjp
def low_back(v):
    return v

def low_keep(v):
    return (low(v), None)

def low_pass(kept, grad):
    return (grad,)

def back_keep(v):
    return (v, None)

def back_low(kept, grad):
    return (low(grad),)
low.defvjp(low_keep, low_pass)
low_back.defvjp(back_keep, back_low)
epsilon = 1e-06
rope_base = 10000.0

def rms_scale(values, gain):
    return values * lax.rsqrt(lax.optimization_barrier(jnp.mean(values * values, axis=-1, keepdims=True)) + epsilon) * gain

def rotary(values, cosine, sine_table):
    halfway = values.shape[-1] // 2
    first = values[..., :halfway]
    second = values[..., halfway:]
    return jnp.concatenate([first * cosine - second * sine_table, second * cosine + first * sine_table], axis=-1)

def rotary_tables(positions):
    halfway = HD // 2
    inverse = rope_base ** (-(jnp.arange(halfway, dtype=jnp.float32) * 2.0 / HD))
    angles = positions.astype(jnp.float32)[:, None] * inverse[None, :]
    return (jnp.cos(angles), jnp.sin(angles))

def matmul(left, right):
    return jnp.dot(left, right, precision=lax.Precision.HIGHEST, preferred_element_type=jnp.float32)

def attend(query, key_rows, value_rows, segments):
    total = query.shape[0]
    span = min(512, total)
    scale = HD ** (-0.5)
    padding = jnp.zeros((WINDOW, HD), jnp.float32)
    all_keys = jnp.concatenate([padding, key_rows])
    all_values = jnp.concatenate([padding, value_rows])
    key_segs = jnp.concatenate([jnp.full((WINDOW,), -1, jnp.int32), segments])
    offsets = jnp.arange(span, dtype=jnp.int32)[:, None] + WINDOW - jnp.arange(span + WINDOW, dtype=jnp.int32)[None, :]
    in_window = (offsets >= 0) & (offsets < WINDOW)

    def one_block(start):
        q_rows = lax.dynamic_slice_in_dim(query, start, span, 0)
        k_rows = lax.dynamic_slice_in_dim(all_keys, start, span + WINDOW, 0)
        v_rows = lax.dynamic_slice_in_dim(all_values, start, span + WINDOW, 0)
        q_segs = lax.dynamic_slice_in_dim(segments, start, span, 0)
        k_segs = lax.dynamic_slice_in_dim(key_segs, start, span + WINDOW, 0)
        allowed = in_window & (q_segs[:, None] == k_segs[None, :])
        raw = low_back(scale * jnp.einsum('qhd,kd->hqk', q_rows, k_rows, precision=lax.Precision.HIGHEST))
        raw = jnp.where(allowed[None], raw, -1e+30)
        peak = lax.optimization_barrier(jnp.max(raw, axis=-1, keepdims=True))
        expo = jnp.exp(raw - peak)
        probs = low(expo / lax.optimization_barrier(jnp.sum(expo, axis=-1, keepdims=True)))
        return jnp.einsum('hqk,kd->qhd', probs, v_rows, precision=lax.Precision.HIGHEST)
    starts = jnp.arange(total // span, dtype=jnp.int32) * span
    result = lax.map(jax.checkpoint(one_block), starts)
    return result.reshape(total, NH * HD)

def reference(hidden_in, segments, w_query, w_key, w_value, w_out, w_gate, w_up, w_down, norm_gains, cotangent):
    total = hidden_in.shape[0]
    index = jnp.arange(total, dtype=jnp.int32)
    is_start = jnp.concatenate([jnp.ones((1,), dtype=bool), segments[1:] != segments[:-1]])
    first_index = lax.cummax(jnp.where(is_start, index, 0), axis=0)
    positions = index - first_index
    cosine, sine_table = rotary_tables(positions)

    def layer(inputs, wq_flat, wk_flat, wv_flat, wo_flat, wg_flat, wu_flat, wd_flat, gain_all):
        w_q = wq_flat.reshape(D, NH * HD)
        w_k = wk_flat.reshape(D, HD)
        w_v = wv_flat.reshape(D, HD)
        w_o = wo_flat.reshape(NH * HD, D)
        w_g = wg_flat.reshape(D, FF)
        w_u = wu_flat.reshape(D, FF)
        w_d = wd_flat.reshape(FF, D)
        gain_in = gain_all[0:D]
        gain_mid = gain_all[D:2 * D]
        gain_pre = gain_all[2 * D:3 * D]
        gain_post = gain_all[3 * D:4 * D]
        gain_query = gain_all[4 * D:4 * D + HD]
        gain_key = gain_all[4 * D + HD:]
        normed = low(rms_scale(inputs, gain_in))
        query_raw = low_back(matmul(normed, w_q)).reshape(total, NH, HD)
        key_raw = low_back(matmul(normed, w_k))
        value_rows = low(low_back(matmul(normed, w_v)))
        query = low(rotary(rms_scale(query_raw, gain_query), cosine[:, None, :], sine_table[:, None, :]))
        key_rows = low(rotary(rms_scale(key_raw, gain_key), cosine, sine_table))
        attended = low(low_back(attend(query, key_rows, value_rows, segments)))
        attn_out = low_back(matmul(attended, w_o))
        middle = inputs + rms_scale(attn_out, gain_mid)
        normed_mid = low(rms_scale(middle, gain_pre))
        gate = low_back(matmul(normed_mid, w_g))
        upward = low_back(matmul(normed_mid, w_u))
        inner = low(jax.nn.gelu(gate, approximate=True) * upward)
        ffn_out = low_back(matmul(inner, w_d))
        return middle + rms_scale(ffn_out, gain_post)
    floats = [item.astype(jnp.float32) for item in (hidden_in, w_query, w_key, w_value, w_out, w_gate, w_up, w_down, norm_gains)]
    result, backward = jax.vjp(layer, *floats)
    grads = backward(cotangent.astype(jnp.float32))
    return (result.astype(jnp.bfloat16), grads[0].astype(jnp.bfloat16), grads[1], grads[2], grads[3], grads[4], grads[5], grads[6], grads[7], grads[8])
```

```python
import jax
import jax.numpy as jnp
from jax import lax
from jax.sharding import PartitionSpec as P

D = 640
NH = 4
HD = 256
FF = 2048
WINDOW = 512


epsilon = 1e-06
rope_base = 10000.0


def shifted(block, axis, distance):
    devices = range(lax.axis_size(axis))
    route = [(i - distance, i) for i in devices if i - distance in devices]
    return lax.ppermute(block, axis, route)


def rms_scale(values, gain):
    return values * lax.rsqrt(jnp.mean(values * values, axis=-1, keepdims=True) + epsilon) * gain


def rotary(values, cosine, sine_table):
    halfway = values.shape[-1] // 2
    first = values[..., :halfway]
    second = values[..., halfway:]
    return jnp.concatenate(
        [first * cosine - second * sine_table, second * cosine + first * sine_table], axis=-1
    )


def rotary_tables(positions):
    halfway = HD // 2
    inverse = rope_base ** (-(jnp.arange(halfway, dtype=jnp.float32) * 2.0 / HD))
    angles = positions.astype(jnp.float32)[:, None] * inverse[None, :]
    return (jnp.cos(angles), jnp.sin(angles))


def outer_sum(left, right):
    return lax.dot_general(
        left, right, (((0,), (0,)), ((), ())), preferred_element_type=jnp.float32
    )


def times_transposed(left, weight):
    return lax.dot_general(
        left, weight, (((1,), (1,)), ((), ())), preferred_element_type=jnp.float32
    )


def forward_dot(left, weight):
    return jnp.dot(left, weight, preferred_element_type=jnp.float32)


def geglu(gate, upward):
    return jax.nn.gelu(gate, approximate=True) * upward


def unpack(pieces):
    return (
        pieces[0].reshape(D, NH * HD),
        pieces[1].reshape(D, HD),
        pieces[2].reshape(D, HD),
        pieces[3].reshape(NH * HD, D),
        pieces[4].reshape(D, FF),
        pieces[5].reshape(D, FF),
        pieces[6].reshape(FF, D),
    )


def gather_packed(shards):
    packed = jnp.concatenate(shards)
    packed = jnp.pad(packed, (0, -packed.shape[0] % 1024)).reshape(-1, 128)
    joined = lax.all_gather(packed, "flat", axis=0, tiled=False)
    joined = joined.reshape(joined.shape[0], -1)
    parts = []
    start = 0
    for shard in shards:
        parts.append(joined[:, start : start + shard.shape[0]].reshape(-1))
        start += shard.shape[0]
    return tuple(parts)


def scatter_packed(grads):
    count = lax.axis_size("flat")
    rows = [grad.astype(jnp.bfloat16).reshape(count, -1) for grad in grads]
    packed = jnp.concatenate(rows, axis=1)
    joined = jnp.pad(packed, ((0, 0), (0, -packed.shape[1] % 2048))).reshape(count, -1, 128)
    own = lax.psum_scatter(joined, "flat", scatter_dimension=0, tiled=False).reshape(-1)
    parts = []
    start = 0
    for row in rows:
        parts.append(own[start : start + row.shape[1]].astype(jnp.float32))
        start += row.shape[1]
    return tuple(parts)


def per_device(
    hidden_in, segments, w_query, w_key, w_value, w_out, w_gate, w_up, w_down, norm_gains, cotangent
):
    tok_rows = hidden_in.shape[0]
    flat_weights = (w_query, w_key, w_value, w_out, w_gate, w_up, w_down, norm_gains)
    gathered = gather_packed(flat_weights[:4] + flat_weights[7:])
    late = gather_packed(flat_weights[4:7])
    gathered = gathered[:4] + late + gathered[4:]
    mat_query, mat_key, mat_value, mat_out, mat_gate, mat_up, mat_down = unpack(gathered)
    gain_all = gathered[7].astype(jnp.float32)
    gain_in = gain_all[0:D]
    gain_mid = gain_all[D : 2 * D]
    gain_pre = gain_all[2 * D : 3 * D]
    gain_post = gain_all[3 * D : 4 * D]
    gain_query = gain_all[4 * D : 4 * D + HD]
    gain_key = gain_all[4 * D + HD :]
    index = jnp.arange(tok_rows, dtype=jnp.int32)
    own_start = jnp.concatenate([jnp.zeros((1,), dtype=bool), segments[1:] != segments[:-1]])
    own_run = lax.cummax(jnp.where(own_start, index, -1), axis=0)
    next_position = tok_rows - own_run[tok_rows - 1 :]
    prev_tail, prev_next = shifted((segments[tok_rows - WINDOW :] + 1, next_position), "flat", 1)
    prev_segs = prev_tail - 1
    starts_here = jnp.concatenate([segments[0:1] != prev_segs[WINDOW - 1 :], own_start[1:]])
    doc_run = lax.cummax(jnp.where(starts_here, index, -1), axis=0)
    positions = jnp.where(doc_run >= 0, index - doc_run, index + prev_next[0])
    cosine, sine_table = rotary_tables(positions)
    inputs = hidden_in.astype(jnp.float32)
    normed, norm_back = jax.vjp(rms_scale, inputs, gain_in)
    normed_b = normed.astype(jnp.bfloat16)
    query_raw = forward_dot(normed_b, mat_query)
    key_raw = forward_dot(normed_b, mat_key)
    value_b = forward_dot(normed_b, mat_value).astype(jnp.bfloat16)

    def rotate_both(q_raw, k_raw, q_gain, k_gain):
        q_normed = rms_scale(q_raw.reshape(tok_rows, NH, HD), q_gain)
        q_turned = rotary(q_normed, cosine[:, None, :], sine_table[:, None, :])
        k_turned = rotary(rms_scale(k_raw, k_gain), cosine, sine_table)
        return (q_turned, k_turned)

    (query_rot, key_rot), rotate_back = jax.vjp(
        rotate_both, query_raw, key_raw, gain_query, gain_key
    )
    query_b = query_rot.astype(jnp.bfloat16)
    key_b = key_rot.astype(jnp.bfloat16)
    prev_keys, prev_values = shifted(
        (key_b[tok_rows - WINDOW :], value_b[tok_rows - WINDOW :]), "flat", 1
    )
    all_keys = jnp.concatenate([prev_keys, key_b])
    all_values = jnp.concatenate([prev_values, value_b])
    key_segs = jnp.concatenate([prev_segs, segments])
    span = min(512, tok_rows)
    scale = HD ** (-0.5)
    offsets = (
        jnp.arange(span, dtype=jnp.int32)[:, None]
        + WINDOW
        - jnp.arange(span + WINDOW, dtype=jnp.int32)[None, :]
    )
    in_window = (offsets >= 0) & (offsets < WINDOW)

    def block_scores(start):
        allowed = in_window & (
            segments[start : start + span][:, None]
            == key_segs[start : start + span + WINDOW][None, :]
        )
        raw = (
            jnp.einsum(
                "qhd,kd->hqk",
                query_b[start : start + span],
                all_keys[start : start + span + WINDOW],
                preferred_element_type=jnp.float32,
            )
            * scale
        )
        return jnp.where(allowed[None], raw, -1e30)

    kept_stats = []
    attended_parts = []
    for block_number in range(tok_rows // span):
        start = block_number * span
        scores = block_scores(start)
        peak = jnp.max(scores, axis=-1, keepdims=True)
        expo = jnp.exp(scores - peak)
        totals = jnp.sum(expo, axis=-1, keepdims=True)
        probs_b = (expo / totals).astype(jnp.bfloat16)
        attended_parts.append(
            jnp.einsum(
                "hqk,kd->qhd",
                probs_b,
                all_values[start : start + span + WINDOW],
                preferred_element_type=jnp.float32,
            )
        )
        kept_stats.append((peak, totals))
    attended_b = jnp.concatenate(attended_parts).reshape(tok_rows, NH * HD).astype(jnp.bfloat16)
    attn_out = forward_dot(attended_b, mat_out)

    def middle_piece(branch, residual, mid_gain, pre_gain):
        middle = residual + rms_scale(branch, mid_gain)
        return (middle, rms_scale(middle, pre_gain))

    (middle, normed_mid), middle_back = jax.vjp(middle_piece, attn_out, inputs, gain_mid, gain_pre)
    normed_mid_b = normed_mid.astype(jnp.bfloat16)
    gate = forward_dot(normed_mid_b, mat_gate)
    upward = forward_dot(normed_mid_b, mat_up)
    inner, geglu_back = jax.vjp(geglu, gate, upward)
    inner_b = inner.astype(jnp.bfloat16)
    ffn_out = forward_dot(inner_b, mat_down)

    def finish_piece(branch, residual, post_gain):
        return residual + rms_scale(branch, post_gain)

    result, finish_back = jax.vjp(finish_piece, ffn_out, middle, gain_post)
    output = result.astype(jnp.bfloat16)
    grad_result = cotangent.astype(jnp.float32)
    d_ffn, d_middle_direct, d_gain_post = finish_back(grad_result)
    d_ffn_b = d_ffn.astype(jnp.bfloat16)
    grad_down = outer_sum(inner_b, d_ffn_b)
    d_inner = times_transposed(d_ffn_b, mat_down)
    d_gate, d_upward = geglu_back(d_inner)
    d_gate_b = d_gate.astype(jnp.bfloat16)
    d_upward_b = d_upward.astype(jnp.bfloat16)
    grad_gate = outer_sum(normed_mid_b, d_gate_b)
    grad_up = outer_sum(normed_mid_b, d_upward_b)
    d_normed_mid = times_transposed(d_gate_b, mat_gate) + times_transposed(d_upward_b, mat_up)
    d_attn, d_inputs_direct, d_gain_mid, d_gain_pre = middle_back((d_middle_direct, d_normed_mid))
    d_attn_b = d_attn.astype(jnp.bfloat16)
    grad_out = outer_sum(attended_b, d_attn_b)
    d_attended_b = (
        times_transposed(d_attn_b, mat_out).astype(jnp.bfloat16).reshape(tok_rows, NH, HD)
    )
    d_keys = jnp.zeros((tok_rows + WINDOW, HD), jnp.float32)
    d_values = jnp.zeros((tok_rows + WINDOW, HD), jnp.float32)
    d_query_parts = []
    for block_number in range(tok_rows // span):
        start = block_number * span
        scores = block_scores(start)
        peak, totals = kept_stats[block_number]
        probs = jnp.exp(scores - peak) / totals
        probs_b = probs.astype(jnp.bfloat16)
        grad_slice = d_attended_b[start : start + span]
        key_slice = all_keys[start : start + span + WINDOW]
        d_probs = jnp.einsum(
            "qhd,kd->hqk",
            grad_slice,
            all_values[start : start + span + WINDOW],
            preferred_element_type=jnp.float32,
        )
        d_scores_b = (probs * (d_probs - jnp.sum(d_probs * probs, axis=-1, keepdims=True))).astype(
            jnp.bfloat16
        )
        d_query_parts.append(
            jnp.einsum("hqk,kd->qhd", d_scores_b, key_slice, preferred_element_type=jnp.float32)
            * scale
        )
        d_keys = d_keys.at[start : start + span + WINDOW].add(
            jnp.einsum(
                "hqk,qhd->kd",
                d_scores_b,
                query_b[start : start + span],
                preferred_element_type=jnp.float32,
            )
            * scale
        )
        d_values = d_values.at[start : start + span + WINDOW].add(
            jnp.einsum("hqk,qhd->kd", probs_b, grad_slice, preferred_element_type=jnp.float32)
        )
    back_keys, back_values = (
        shifted(d_keys[:WINDOW].astype(jnp.bfloat16), "flat", -1).astype(jnp.float32),
        shifted(d_values[:WINDOW].astype(jnp.bfloat16), "flat", -1).astype(jnp.float32),
    )
    d_key_rot = d_keys[WINDOW:].at[tok_rows - WINDOW :].add(back_keys)
    d_value_all = d_values[WINDOW:].at[tok_rows - WINDOW :].add(back_values)
    d_query_rot = jnp.concatenate(d_query_parts)
    d_query_raw, d_key_raw, d_gain_query, d_gain_key = rotate_back((d_query_rot, d_key_rot))
    d_query_b = d_query_raw.astype(jnp.bfloat16)
    d_key_b = d_key_raw.astype(jnp.bfloat16)
    d_value_b = d_value_all.astype(jnp.bfloat16)
    grad_query = outer_sum(normed_b, d_query_b)
    grad_key = outer_sum(normed_b, d_key_b)
    grad_value = outer_sum(normed_b, d_value_b)
    d_normed = (
        times_transposed(d_query_b, mat_query)
        + times_transposed(d_key_b, mat_key)
        + times_transposed(d_value_b, mat_value)
    )
    d_inputs_norm, d_gain_in = norm_back(d_normed)
    grad_in = (d_inputs_direct + d_inputs_norm).astype(jnp.bfloat16)
    grad_gains = jnp.concatenate(
        [d_gain_in, d_gain_mid, d_gain_pre, d_gain_post, d_gain_query, d_gain_key]
    )
    early = scatter_packed((grad_gate, grad_up, grad_down))
    tail = scatter_packed((grad_query, grad_key, grad_value, grad_out, grad_gains))
    summed = tail[:4] + early + tail[4:]
    return (
        output,
        grad_in,
        summed[0],
        summed[1],
        summed[2],
        summed[3],
        summed[4],
        summed[5],
        summed[6],
        summed[7],
    )


def solution(mesh):
    in_specs = (
        P("flat", None),
        P("flat"),
        P("flat"),
        P("flat"),
        P("flat"),
        P("flat"),
        P("flat"),
        P("flat"),
        P("flat"),
        P("flat"),
        P("flat", None),
    )
    out_specs = (
        P("flat", None),
        P("flat", None),
        P("flat"),
        P("flat"),
        P("flat"),
        P("flat"),
        P("flat"),
        P("flat"),
        P("flat"),
        P("flat"),
    )
    return jax.shard_map(
        per_device, mesh=mesh, in_specs=in_specs, out_specs=out_specs, check_vma=False
    )
```

```python
import functools

import jax
import jax.numpy as jnp
from jax import lax
from jax.experimental import pallas as pl
from jax.experimental.pallas import tpu as pltpu
from jax.sharding import PartitionSpec as P

D = 640
NH = 4
HD = 256
FF = 2048
WINDOW = 512

PIECES = 32
ROWS = D // PIECES
TILE = 256
QKV = (NH + 2) * HD
GROUP = QKV // 4
CHUNK = 512
LANES = 128
HALF = HD // 2
SCALE = HD ** (-0.5)

epsilon = 1e-06
rope_base = 10000.0

bf16 = jnp.bfloat16
f32 = jnp.float32


def params(megabytes):
    return pltpu.CompilerParams(vmem_limit_bytes=megabytes << 20)


def whole(shape, space=None):
    return pl.BlockSpec(shape, lambda i, *_: (0,) * len(shape))


def rows_of(width, first=0):
    return pl.BlockSpec((TILE, width), lambda i, *_: (i + first, 0))


def shifted(block, distance):
    devices = range(lax.axis_size("flat"))
    route = [(i - distance, i) for i in devices if i - distance in devices]
    return lax.ppermute(block, "flat", route)


def swapped(block, mask):
    count = lax.axis_size("flat")
    near = count // PIECES
    route = [(i, ((i // near) ^ mask) * near + i % near) for i in range(count)]
    return lax.ppermute(block, "flat", route)


def gather_relative(shards, orders):
    held = [shard[None] for shard in shards]
    for step in range(len(orders[0])):
        came = [swapped(one, order[step]) for one, order in zip(held, orders)]
        held = [jnp.concatenate(pair) for pair in zip(held, came)]
    return held


def place_table(me, order):
    differ = me ^ jnp.arange(PIECES, dtype=jnp.int32)
    place = jnp.zeros((PIECES,), jnp.int32)
    for step, mask in enumerate(order):
        place = place + jnp.where((differ & mask) != 0, 1 << step, 0)
    return place


def chip_table(me, order):
    differ = (me >> 1) ^ jnp.arange(PIECES // 2, dtype=jnp.int32)
    place = jnp.zeros((PIECES // 2,), jnp.int32)
    for step, mask in enumerate(order):
        place = place + jnp.where((differ & (mask >> 1)) != 0, 1 << (3 - step), 0)
    return jnp.concatenate([place, (me & 1)[None]]).astype(jnp.int32)


def scatter_relative(keeps, sends, orders):
    came = [swapped(one, 1) for one in sends]
    held = [(keep, other) for keep, other in zip(keeps, came)]
    for step in range(4):
        half = 1 << (3 - step)
        nxt = []
        for (keep, other), order in zip(held, orders):
            away = (keep[half:].astype(f32) + other[half:].astype(f32)).astype(bf16)
            stay = (keep[:half].astype(f32) + other[:half].astype(f32)).astype(bf16)
            nxt.append((stay, swapped(away, order[step])))
        held = nxt
    return [(keep.astype(f32) + other.astype(f32))[0] for keep, other in held]


def dot(left, right):
    return lax.dot_general(left, right, (((1,), (0,)), ((), ())), preferred_element_type=f32)


def dot_bt(left, right):
    return lax.dot_general(left, right, (((1,), (1,)), ((), ())), preferred_element_type=f32)


def dot_at(left, right):
    return lax.dot_general(left, right, (((0,), (0,)), ((), ())), preferred_element_type=f32)


def inv_rms(values):
    return lax.rsqrt(jnp.mean(values * values, axis=-1, keepdims=True) + epsilon)


def rms_back(values, inverse, gain, grad):
    scaled = grad * gain
    mean = jnp.mean(scaled * values, axis=-1, keepdims=True)
    return inverse * scaled - values * (inverse * inverse * inverse * mean)


def store_pair(keep, send, index, core, even, odd):
    mine = core == 0
    keep[index] = jnp.where(mine, even, odd).astype(bf16)
    send[index] = jnp.where(mine, odd, even).astype(bf16)


def qkv_kernel(
    tab_ref, tab_out_ref, hidden_ref, gain_ref, head_ref, packed_ref, out_packed_ref, cos_ref, sin_ref,
    query_ref, kv_ref, query_raw_ref, key_raw_ref, weight_ref, out_ref,
):
    @pl.when(pl.program_id(0) == 0)
    def _():
        for d in range(PIECES):
            block = packed_ref[tab_ref[d]]
            for h in range(4):
                weight_ref[ROWS * d : ROWS * (d + 1), GROUP * h : GROUP * (h + 1)] = block[
                    ROWS * h : ROWS * (h + 1)
                ]
            out_ref[32 * d : 32 * (d + 1)] = out_packed_ref[tab_out_ref[d]]

    inputs = hidden_ref[...].astype(f32)
    normed = (inputs * inv_rms(inputs) * gain_ref[0:1]).astype(bf16)
    raw = dot(normed, weight_ref[...])
    cosine = cos_ref[...]
    sine = sin_ref[...]

    def turned(values, gain):
        values = values * inv_rms(values) * gain
        first, second = values[:, :HALF], values[:, HALF:]
        return jnp.concatenate(
            [first * cosine - second * sine, second * cosine + first * sine], axis=1
        )

    for h in range(NH):
        columns = slice(HD * h, HD * (h + 1))
        query_ref[:, columns] = (turned(raw[:, columns], head_ref[0:1]) * SCALE).astype(bf16)
    query_raw_ref[...] = raw[:, : NH * HD]
    key_raw = raw[:, NH * HD : NH * HD + HD]
    key_raw_ref[...] = key_raw
    kv_ref[:, :HD] = turned(key_raw, head_ref[1:2]).astype(bf16)
    kv_ref[:, HD:] = raw[:, NH * HD + HD :].astype(bf16)


def qkv_call(tab, tab_out, hidden, gains, heads, packed, out_packed, cosine, sine):
    tokens = hidden.shape[0]
    return pl.pallas_call(
        qkv_kernel,
        grid_spec=pltpu.PrefetchScalarGridSpec(
            num_scalar_prefetch=2,
            grid=(tokens // TILE,),
            in_specs=[
                rows_of(D), whole((8, D)), whole((8, HD)), whole(packed.shape),
                whole(out_packed.shape), rows_of(HALF), rows_of(HALF),
            ],
            out_specs=[
                rows_of(NH * HD), rows_of(2 * HD), rows_of(NH * HD), rows_of(HD),
                whole((D, QKV)), whole((NH * HD, D)),
            ],
        ),
        out_shape=[
            jax.ShapeDtypeStruct((tokens, NH * HD), bf16),
            jax.ShapeDtypeStruct((tokens, 2 * HD), bf16),
            jax.ShapeDtypeStruct((tokens, NH * HD), f32),
            jax.ShapeDtypeStruct((tokens, HD), f32),
            jax.ShapeDtypeStruct((D, QKV), bf16),
            jax.ShapeDtypeStruct((NH * HD, D), bf16),
        ],
        compiler_params=params(48),
        cost_estimate=pl.CostEstimate(flops=2 * tokens * D * QKV, bytes_accessed=20 << 20, transcendentals=0),
        name="qkv",
    )(tab, tab_out, hidden, gains, heads, packed, out_packed, cosine, sine)


def allowed_keys(spot_ref, first):
    token = lax.broadcasted_iota(jnp.int32, (1, TILE), 1)
    spot = token + first
    position = jnp.where(spot < spot_ref[0], spot + spot_ref[1], spot - spot_ref[0])
    lowest = token + WINDOW - jnp.minimum(position, WINDOW - 1)
    key = lax.broadcasted_iota(jnp.int32, (TILE + WINDOW, TILE), 0)
    return (key >= lowest) & (key <= token + WINDOW)


def attend_kernel(start, spot_ref, query_ref, kv_ref, out_ref, *refs):
    attended_ref, attn_ref, stat_ref = refs[-3:]
    step = pl.program_id(0)
    keys = kv_ref[pl.ds(step * TILE, TILE + WINDOW), :HD]
    values = kv_ref[pl.ds(step * TILE, TILE + WINDOW), HD:]
    values_t = values.T
    allowed = allowed_keys(spot_ref, start + step * TILE)
    for h in range(NH):
        columns = slice(HD * h, HD * (h + 1))
        scores = dot_bt(keys, query_ref[:, columns])
        expo = jnp.where(allowed, jnp.exp(scores), 0.0)
        total = jnp.sum(expo, axis=0, keepdims=True)
        mixed = dot(values_t, expo.astype(bf16)) * (1.0 / total)
        attended_ref[:, columns] = mixed.T.astype(bf16)
        stat_ref[h : h + 1, :] = jnp.log(total)
    attn_ref[...] = dot(attended_ref[...], out_ref[...])


def attend_call(start, spot, query, kv, out, kept):
    tokens = query.shape[0]
    first = start // TILE
    outs = [
        jax.ShapeDtypeStruct((tokens, NH * HD), bf16),
        jax.ShapeDtypeStruct((tokens, D), f32),
        jax.ShapeDtypeStruct((8, tokens), f32),
    ]
    return pl.pallas_call(
        functools.partial(attend_kernel, start),
        grid_spec=pltpu.PrefetchScalarGridSpec(
            num_scalar_prefetch=1,
            grid=(2,),
            in_specs=[rows_of(NH * HD, first), whole(kv.shape), whole(out.shape)]
            + [pl.BlockSpec(memory_space=pl.ANY)] * len(kept),
            out_specs=[
                rows_of(NH * HD, first),
                rows_of(D, first),
                pl.BlockSpec((8, TILE), lambda i, *_: (0, i + first)),
            ],
        ),
        out_shape=outs,
        input_output_aliases={4 + i: i for i in range(len(kept))},
        compiler_params=params(48),
        cost_estimate=pl.CostEstimate(flops=5 << 30, bytes_accessed=8 << 20, transcendentals=1 << 21),
        name="attend",
    )(spot, query, kv, out, *kept)


def ffn_kernel(
    tab_ref, hidden_ref, attn_ref, cot_ref, gain_ref, packed_ref, down_ref,
    output_ref, dmid_ref, dattn_ref, dgain_ref, keep_ref, send_ref, down_keep_ref, down_send_ref,
    middle_ref, normed_ref, normed_t_ref, sum_ref, dffn_ref, gate_w, up_w, down_w, inner_ref, slope_ref, act_ref,
):
    step = pl.program_id(0)
    tokens = hidden_ref.shape[0]
    parts = tokens // TILE
    chunks = FF // CHUNK
    core = tab_ref[PIECES // 2]

    @pl.when(step == 0)
    def _():
        def one(part, _):
            rows = pl.ds(pl.multiple_of(part * TILE, TILE), TILE)
            branch = attn_ref[rows]
            middle = hidden_ref[rows].astype(f32) + branch * inv_rms(branch) * gain_ref[1:2]
            middle_ref[rows] = middle
            normed_ref[rows] = (middle * inv_rms(middle) * gain_ref[2:3]).astype(bf16)
            return 0

        lax.fori_loop(0, parts, one, 0)
        normed_t_ref[...] = normed_ref[...].T

    @pl.when(step < chunks)
    def _():
        for d in range(PIECES):
            for j in range(CHUNK // LANES):
                columns = slice(LANES * j, LANES * (j + 1))
                rows = slice(ROWS * d, ROWS * (d + 1))
                gate_w[step, rows, columns] = packed_ref[d, ROWS * j : ROWS * (j + 1)]
                up_w[step, rows, columns] = packed_ref[d, 80 + ROWS * j : 80 + ROWS * (j + 1)]
        for i in range(CHUNK // 64):
            for g in range(D // LANES):
                down_w[step, 64 * i : 64 * (i + 1), LANES * g : LANES * (g + 1)] = down_ref[
                    i, 64 * g : 64 * (g + 1)
                ]
        for part in range(parts):
            rows = slice(part * TILE, (part + 1) * TILE)
            gate = dot(normed_ref[rows], gate_w[step])
            upward = dot(normed_ref[rows], up_w[step])
            square = gate * gate
            c0 = 0.7978845608028654
            c1 = c0 * 0.044715
            half = 0.5 * jnp.tanh(gate * (c0 + c1 * square)) + 0.5
            active = gate * half
            slope = half + 2.0 * active * (1.0 - half) * (c0 + 3.0 * c1 * square)
            inner = (active * upward).astype(bf16)
            inner_ref[step, rows] = inner
            act_ref[step, rows] = active.astype(bf16)
            slope_ref[step, rows] = (slope * upward).astype(bf16)
            more = dot(inner, down_w[step])

            @pl.when(step == 0)
            def _():
                sum_ref[rows] = more

            @pl.when(step > 0)
            def _():
                sum_ref[rows] += more

    @pl.when(step == chunks - 1)
    def _():
        def one(part, total):
            rows = pl.ds(pl.multiple_of(part * TILE, TILE), TILE)
            branch = sum_ref[rows]
            inverse = inv_rms(branch)
            grad = cot_ref[rows].astype(f32)
            output_ref[rows] = (middle_ref[rows] + branch * inverse * gain_ref[3:4]).astype(bf16)
            dffn_ref[rows] = rms_back(branch, inverse, gain_ref[3:4], grad).astype(bf16)
            return total + jnp.sum(grad * branch * inverse, axis=0, keepdims=True)

        dgain_ref[...] = jnp.zeros_like(dgain_ref)
        dgain_ref[3:4] = lax.fori_loop(0, parts, one, jnp.zeros((1, D), f32))

    @pl.when(step >= chunks)
    def _():
        chunk = step - chunks
        d_inner = dot_bt(dffn_ref[...], down_w[chunk])
        d_gate = (d_inner * slope_ref[chunk].astype(f32)).astype(bf16)
        d_up = (d_inner * act_ref[chunk].astype(f32)).astype(bf16)
        more = dot_bt(d_gate, gate_w[chunk]) + dot_bt(d_up, up_w[chunk])

        @pl.when(chunk == 0)
        def _():
            sum_ref[...] = more

        @pl.when(chunk > 0)
        def _():
            sum_ref[...] += more

        for which, grad_in in ((0, d_gate), (1, d_up)):
            for j in range(CHUNK // LANES // 2):
                grad = dot(normed_t_ref[...], grad_in[:, 256 * j : 256 * (j + 1)])
                for k in range(2):
                    low = 80 * which + ROWS * (2 * j + k)
                    for e in range(PIECES // 2):
                        even = grad[2 * ROWS * e : 2 * ROWS * e + ROWS, LANES * k : LANES * (k + 1)]
                        odd = grad[2 * ROWS * e + ROWS : 2 * ROWS * (e + 1), LANES * k : LANES * (k + 1)]
                        mine = core == 0
                        place = tab_ref[e]
                        keep_ref[place, 0, low : low + ROWS] = jnp.where(mine, even, odd).astype(bf16)
                        send_ref[place, 0, low : low + ROWS] = jnp.where(mine, odd, even).astype(bf16)
        grad = dot_at(inner_ref[chunk], dffn_ref[...])
        for i in range(CHUNK // 128):
            place = tab_ref[chunk * (CHUNK // 128) + i]
            store_pair(
                down_keep_ref, down_send_ref, place, core,
                grad[128 * i : 128 * i + 64], grad[128 * i + 64 : 128 * (i + 1)],
            )

    @pl.when(step == 2 * chunks - 1)
    def _():
        def one(part, totals):
            rows = pl.ds(pl.multiple_of(part * TILE, TILE), TILE)
            middle = middle_ref[rows]
            inverse = inv_rms(middle)
            grad = sum_ref[rows]
            d_mid = cot_ref[rows].astype(f32) + rms_back(middle, inverse, gain_ref[2:3], grad)
            pre = jnp.sum(grad * middle * inverse, axis=0, keepdims=True)
            branch = attn_ref[rows]
            inverse = inv_rms(branch)
            dmid_ref[rows] = d_mid
            dattn_ref[rows] = rms_back(branch, inverse, gain_ref[1:2], d_mid).astype(bf16)
            mid = jnp.sum(d_mid * branch * inverse, axis=0, keepdims=True)
            return totals[0] + mid, totals[1] + pre

        zero = jnp.zeros((1, D), f32)
        mid, pre = lax.fori_loop(0, parts, one, (zero, zero))
        dgain_ref[1:2] = mid
        dgain_ref[2:3] = pre


def ffn_call(tab, hidden, attn_out, cotangent, gains, packed):
    tokens = hidden.shape[0]
    chunks = FF // CHUNK
    pairs = PIECES // 2
    once = pl.Buffered(1)

    def single(shape):
        return pl.BlockSpec(shape, lambda i, *_: (0,) * len(shape), pipeline_mode=once)

    return pl.pallas_call(
        ffn_kernel,
        grid_spec=pltpu.PrefetchScalarGridSpec(
            num_scalar_prefetch=1,
            grid=(2 * chunks,),
            in_specs=[
                single((tokens, D)), single((tokens, D)), single((tokens, D)), whole((8, D)),
                pl.BlockSpec((PIECES, 160, LANES), lambda i, *_: (0, jnp.minimum(i, chunks - 1), 0)),
                pl.BlockSpec((8, 320, LANES), lambda i, *_: (jnp.minimum(i, chunks - 1), 2, 0)),
            ],
            out_specs=[
                single((tokens, D)), single((tokens, D)), single((tokens, D)), whole((8, D)),
                pl.BlockSpec((pairs, 1, 160, LANES), lambda i, *_: (0, jnp.maximum(i - chunks, 0), 0, 0)),
                pl.BlockSpec((pairs, 1, 160, LANES), lambda i, *_: (0, jnp.maximum(i - chunks, 0), 0, 0)),
                single((pairs, 64, D)), single((pairs, 64, D)),
            ],
            scratch_shapes=[
                pltpu.VMEM((tokens, D), f32),
                pltpu.VMEM((tokens, D), bf16),
                pltpu.VMEM((D, tokens), bf16),
                pltpu.VMEM((tokens, D), f32),
                pltpu.VMEM((tokens, D), bf16),
                pltpu.VMEM((chunks, D, CHUNK), bf16),
                pltpu.VMEM((chunks, D, CHUNK), bf16),
                pltpu.VMEM((chunks, CHUNK, D), bf16),
                pltpu.VMEM((chunks, tokens, CHUNK), bf16),
                pltpu.VMEM((chunks, tokens, CHUNK), bf16),
                pltpu.VMEM((chunks, tokens, CHUNK), bf16),
            ],
        ),
        out_shape=[
            jax.ShapeDtypeStruct((tokens, D), bf16),
            jax.ShapeDtypeStruct((tokens, D), f32),
            jax.ShapeDtypeStruct((tokens, D), bf16),
            jax.ShapeDtypeStruct((8, D), f32),
            jax.ShapeDtypeStruct((pairs, chunks, 160, LANES), bf16),
            jax.ShapeDtypeStruct((pairs, chunks, 160, LANES), bf16),
            jax.ShapeDtypeStruct((pairs, 64, D), bf16),
            jax.ShapeDtypeStruct((pairs, 64, D), bf16),
        ],
        compiler_params=params(60),
        cost_estimate=pl.CostEstimate(flops=18 * tokens * D * FF, bytes_accessed=30 << 20, transcendentals=tokens * FF),
        name="feed_forward",
    )(tab, hidden, attn_out, cotangent, gains, packed, packed)


def out_kernel(tab_ref, dattn_ref, out_ref, attended_ref, datt_ref, keep_ref, send_ref):
    core = tab_ref[PIECES // 2]
    datt_ref[...] = dot_bt(dattn_ref[...], out_ref[...]).astype(bf16)
    for b in range(NH * HD // 256):
        grad = dot_at(attended_ref[:, 256 * b : 256 * (b + 1)], dattn_ref[...])
        for i in range(4):
            store_pair(
                keep_ref, send_ref, tab_ref[4 * b + i], core,
                grad[64 * i : 64 * i + 32], grad[64 * i + 32 : 64 * (i + 1)],
            )


def out_call(tab, d_attn, out, attended):
    tokens = d_attn.shape[0]
    pairs = PIECES // 2
    return pl.pallas_call(
        out_kernel,
        grid_spec=pltpu.PrefetchScalarGridSpec(
            num_scalar_prefetch=1,
            grid=(1,),
            in_specs=[whole(d_attn.shape), whole(out.shape), whole(attended.shape)],
            out_specs=[whole((tokens, NH * HD)), whole((pairs, 32, D)), whole((pairs, 32, D))],
        ),
        out_shape=[
            jax.ShapeDtypeStruct((tokens, NH * HD), bf16),
            jax.ShapeDtypeStruct((pairs, 32, D), bf16),
            jax.ShapeDtypeStruct((pairs, 32, D), bf16),
        ],
        compiler_params=params(48),
        cost_estimate=pl.CostEstimate(flops=4 * tokens * D * NH * HD, bytes_accessed=8 << 20, transcendentals=0),
        name="out_backward",
    )(tab, d_attn, out, attended)


def attend_back_kernel(
    start, spot_ref, query_ref, kv_ref, datt_ref, stat_ref, raw_ref, cos_ref, sin_ref, head_ref, *refs
):
    dquery_ref, dgain_ref, dkv_ref = refs[-3:]
    step = pl.program_id(0)

    @pl.when(step == 0)
    def _():
        dkv_ref[...] = jnp.zeros_like(dkv_ref)
        dgain_ref[...] = jnp.zeros_like(dgain_ref)

    span = pl.ds(step * TILE, TILE + WINDOW)
    keys = kv_ref[span, :HD]
    values = kv_ref[span, HD:]
    keys_t = keys.T
    allowed = allowed_keys(spot_ref, start + step * TILE)
    cosine = cos_ref[...]
    sine = sin_ref[...]
    gain = head_ref[0:1]
    d_gain = jnp.zeros((1, HD), f32)
    for h in range(NH):
        columns = slice(HD * h, HD * (h + 1))
        query = query_ref[:, columns]
        grad = datt_ref[:, columns]
        scores = dot_bt(keys, query) - stat_ref[h : h + 1, :]
        probs = jnp.where(allowed, jnp.exp(scores), 0.0)
        d_probs = dot_bt(values, grad)
        inside = jnp.sum(probs * d_probs, axis=0, keepdims=True)
        d_scores = (probs * (d_probs - inside)).astype(bf16)
        dkv_ref[span, HD:] += dot(probs.astype(bf16), grad)
        dkv_ref[span, :HD] += dot(d_scores, query)
        turned = dot(keys_t, d_scores).T * SCALE
        first, second = turned[:, :HALF], turned[:, HALF:]
        turned = jnp.concatenate(
            [first * cosine + second * sine, second * cosine - first * sine], axis=1
        )
        raw = raw_ref[:, columns]
        inverse = inv_rms(raw)
        dquery_ref[:, columns] = rms_back(raw, inverse, gain, turned).astype(bf16)
        d_gain = d_gain + jnp.sum(turned * raw * inverse, axis=0, keepdims=True)
    dgain_ref[0:1] += d_gain


def attend_back_call(start, spot, query, kv, d_attended, stat, query_raw, cosine, sine, heads, kept):
    tokens = query.shape[0]
    first = start // TILE
    return pl.pallas_call(
        functools.partial(attend_back_kernel, start),
        grid_spec=pltpu.PrefetchScalarGridSpec(
            num_scalar_prefetch=1,
            grid=(2,),
            in_specs=[
                rows_of(NH * HD, first), whole(kv.shape), rows_of(NH * HD, first),
                pl.BlockSpec((8, TILE), lambda i, *_: (0, i + first)),
                rows_of(NH * HD, first), rows_of(HALF, first), rows_of(HALF, first), whole((8, HD)),
            ]
            + [pl.BlockSpec(memory_space=pl.ANY)] * len(kept),
            out_specs=[rows_of(NH * HD, first), whole((8, HD)), whole(kv.shape)],
        ),
        out_shape=[
            jax.ShapeDtypeStruct((tokens, NH * HD), bf16),
            jax.ShapeDtypeStruct((8, HD), f32),
            jax.ShapeDtypeStruct(kv.shape, f32),
        ],
        input_output_aliases={9 + i: i for i in range(len(kept))},
        compiler_params=params(48),
        cost_estimate=pl.CostEstimate(flops=9 << 30, bytes_accessed=10 << 20, transcendentals=1 << 21),
        name="attend_backward",
    )(spot, query, kv, d_attended, stat, query_raw, cosine, sine, heads, *kept)


def qkv_back_kernel(
    tab_ref, hidden_ref, gain_ref, head_ref, dquery_ref, near_ref, early_ref, halo_ref, key_raw_ref,
    cos_ref, sin_ref, weight_ref, dmid_ref, dffn_gain_ref, dhead0_ref, dhead1_ref,
    grad_ref, keep_ref, send_ref, normed_ref, dqkv_ref, din_ref, dkey_ref,
):
    step = pl.program_id(0)
    rows = pl.ds(pl.multiple_of(step * TILE, TILE), TILE)
    core = tab_ref[PIECES // 2]

    @pl.when(step == 0)
    def _():
        din_ref[...] = jnp.zeros_like(din_ref)
        dkey_ref[...] = jnp.zeros_like(dkey_ref)

    inputs = hidden_ref[...].astype(f32)
    inverse = inv_rms(inputs)
    normed_ref[rows] = (inputs * inverse * gain_ref[0:1]).astype(bf16)
    d_kv = near_ref[...] + jnp.where(step < 2, early_ref[...], halo_ref[...].astype(f32))
    cosine = cos_ref[...]
    sine = sin_ref[...]
    first, second = d_kv[:, :HALF], d_kv[:, HALF:HD]
    turned = jnp.concatenate(
        [first * cosine + second * sine, second * cosine - first * sine], axis=1
    )
    raw = key_raw_ref[...]
    raw_inverse = inv_rms(raw)
    dkey_ref[0:1] += jnp.sum(turned * raw * raw_inverse, axis=0, keepdims=True)
    dqkv_ref[rows, : NH * HD] = dquery_ref[...]
    dqkv_ref[rows, NH * HD : NH * HD + HD] = rms_back(raw, raw_inverse, head_ref[1:2], turned).astype(bf16)
    dqkv_ref[rows, NH * HD + HD :] = d_kv[:, HD:].astype(bf16)
    d_normed = dot_bt(dqkv_ref[rows], weight_ref[...])
    din_ref[0:1] += jnp.sum(d_normed * inputs * inverse, axis=0, keepdims=True)
    grad_ref[...] = (dmid_ref[...] + rms_back(inputs, inverse, gain_ref[0:1], d_normed)).astype(bf16)

    @pl.when(step == pl.num_programs(0) - 1)
    def _():
        for h in range(4):
            grad = dot_at(normed_ref[...], dqkv_ref[:, GROUP * h : GROUP * (h + 1)])
            for e in range(PIECES // 2):
                even = grad[2 * ROWS * e : 2 * ROWS * e + ROWS]
                odd = grad[2 * ROWS * e + ROWS : 2 * ROWS * (e + 1)]
                place = tab_ref[e]
                mine = core == 0
                keep_ref[place, ROWS * h : ROWS * (h + 1)] = jnp.where(mine, even, odd).astype(bf16)
                send_ref[place, ROWS * h : ROWS * (h + 1)] = jnp.where(mine, odd, even).astype(bf16)
        gains = jnp.concatenate(
            [
                din_ref[0:1], dffn_gain_ref[1:2], dffn_gain_ref[2:3], dffn_gain_ref[3:4],
                dhead0_ref[0:1] + dhead1_ref[0:1], dkey_ref[0:1],
            ],
            axis=1,
        )
        piece = gains.shape[1] // PIECES
        mine = core == 0
        for e in range(PIECES // 2):
            even = jnp.broadcast_to(gains[:, 2 * piece * e : 2 * piece * e + piece], (8, piece))
            odd = jnp.broadcast_to(gains[:, 2 * piece * e + piece : 2 * piece * (e + 1)], (8, piece))
            place = tab_ref[e]
            keep_ref[place, 80:88] = jnp.zeros((8, GROUP), bf16)
            send_ref[place, 80:88] = jnp.zeros((8, GROUP), bf16)
            keep_ref[place, 80:88, 0:piece] = jnp.where(mine, even, odd).astype(bf16)
            send_ref[place, 80:88, 0:piece] = jnp.where(mine, odd, even).astype(bf16)


def qkv_back_call(
    tab, hidden, gains, heads, d_query, near, early, halo, key_raw, cosine, sine, weight, d_mid,
    d_gains, d_head0, d_head1,
):
    tokens = hidden.shape[0]
    pairs = PIECES // 2
    last = WINDOW // TILE
    return pl.pallas_call(
        qkv_back_kernel,
        grid_spec=pltpu.PrefetchScalarGridSpec(
            num_scalar_prefetch=1,
            grid=(tokens // TILE,),
            in_specs=[
                rows_of(D), whole((8, D)), whole((8, HD)), rows_of(NH * HD), rows_of(2 * HD),
                pl.BlockSpec((TILE, 2 * HD), lambda i, *_: (jnp.minimum(i + last, 2 * last - 1), 0)),
                pl.BlockSpec((TILE, 2 * HD), lambda i, *_: (jnp.clip(i - last, 0, last - 1), 0)),
                rows_of(HD), rows_of(HALF), rows_of(HALF), whole((D, QKV)), rows_of(D),
                whole((8, D)), whole((8, HD)), whole((8, HD)),
            ],
            out_specs=[rows_of(D), whole((pairs, 88, GROUP)), whole((pairs, 88, GROUP))],
            scratch_shapes=[
                pltpu.VMEM((tokens, D), bf16),
                pltpu.VMEM((tokens, QKV), bf16),
                pltpu.VMEM((8, D), f32),
                pltpu.VMEM((8, HD), f32),
            ],
        ),
        out_shape=[
            jax.ShapeDtypeStruct((tokens, D), bf16),
            jax.ShapeDtypeStruct((pairs, 88, GROUP), bf16),
            jax.ShapeDtypeStruct((pairs, 88, GROUP), bf16),
        ],
        compiler_params=params(48),
        cost_estimate=pl.CostEstimate(flops=4 * tokens * D * QKV, bytes_accessed=16 << 20, transcendentals=0),
        name="qkv_backward",
    )(
        tab, hidden, gains, heads, d_query, near, early, halo, key_raw, cosine, sine, weight, d_mid,
        d_gains, d_head0, d_head1,
    )


def rotary_tables(positions):
    inverse = rope_base ** (-(jnp.arange(HALF, dtype=f32) * 2.0 / HD))
    angles = positions.astype(f32)[:, None] * inverse[None, :]
    return (jnp.cos(angles), jnp.sin(angles))


def per_device(
    hidden_in, segments, w_query, w_key, w_value, w_out, w_gate, w_up, w_down, norm_gains, cotangent
):
    tokens = hidden_in.shape[0]
    count = lax.axis_size("flat")
    near = count // PIECES
    me = lax.axis_index("flat") // near
    groups = [[p * near + i for i in range(near)] for p in range(PIECES)]
    shards = (w_query, w_key, w_value, w_out, w_gate, w_up, w_down, norm_gains)
    if near > 1:
        shards = [
            lax.all_gather(one, "flat", axis=0, tiled=True, axis_index_groups=groups) for one in shards
        ]
    s_query, s_key, s_value, s_out, s_gate, s_up, s_down, s_gain = shards

    gate_up = jnp.stack([s_gate.reshape(ROWS, -1, 4, LANES), s_up.reshape(ROWS, -1, 4, LANES)], axis=2)
    gate_up = gate_up.transpose(1, 2, 3, 0, 4).reshape(-1, LANES)
    down = s_down.reshape(-1, D // LANES, LANES).transpose(1, 0, 2).reshape(-1, LANES)
    late = jnp.concatenate([gate_up, down])
    if near > 1:
        columns = [[p * near + i for p in range(PIECES)] for i in range(near)]
        ffn_packed = lax.all_gather(late, "flat", axis=0, tiled=False, axis_index_groups=columns)
    else:
        ffn_packed = lax.all_gather(late, "flat", axis=0, tiled=False)

    qkv = jnp.concatenate(
        [s_query.reshape(ROWS, -1), s_key.reshape(ROWS, -1), s_value.reshape(ROWS, -1)], axis=1
    )
    gain_row = jnp.pad(s_gain[None], ((0, 7), (0, GROUP - s_gain.shape[0])))
    qkv = jnp.concatenate([qkv[:, GROUP * h : GROUP * (h + 1)] for h in range(4)] + [gain_row])
    order_qkv = (16, 8, 2, 4, 1)
    order_out = (16, 8, 4, 2, 1)
    qkv_packed, out_packed = gather_relative([qkv, s_out.reshape(-1, D)], [order_qkv, order_out])
    tab_qkv = place_table(me, order_qkv)
    tab_out = place_table(me, order_out)
    gain_all = jnp.take(qkv_packed[:, 80, : s_gain.shape[0]], tab_qkv, axis=0).astype(f32).reshape(-1)
    gains = jnp.pad(gain_all[: 4 * D].reshape(4, D), ((0, 4), (0, 0)))
    heads = jnp.pad(gain_all[4 * D :].reshape(2, HD), ((0, 6), (0, 0)))

    rise = jnp.sum((segments == segments[0]).astype(jnp.int32))
    told = shifted(jnp.stack([segments[tokens - 1] + 1, tokens - rise]), 1)
    ahead = jnp.where(told[0] == segments[0] + 1, told[1], 0)
    index = jnp.arange(tokens, dtype=jnp.int32)
    positions = jnp.where(index < rise, index + ahead, index - rise)
    spot = jnp.stack([rise, ahead]).astype(jnp.int32)
    cosine, sine = rotary_tables(positions)

    query, kv, query_raw, key_raw, weight, out = qkv_call(
        tab_qkv, tab_out, hidden_in, gains, heads, qkv_packed, out_packed, cosine, sine
    )
    kv_prev = shifted(kv[tokens - WINDOW :], 1)
    upper = attend_call(tokens - 2 * TILE, spot, query, kv, out, ())
    kv_low = jnp.concatenate([kv_prev, kv[: tokens - WINDOW]])
    attended, attn_out, stat = attend_call(0, spot, query, kv_low, out, upper)

    route_a = (2, 4, 8, 16)
    route_b = (4, 2, 8, 16)
    tab_a = chip_table(me, route_a)
    tab_b = chip_table(me, route_b)
    output, d_mid, d_attn, d_gains, keep_ff, send_ff, keep_down, send_down = ffn_call(
        tab_a, hidden_in, attn_out, cotangent, gains, ffn_packed
    )
    d_attended, keep_out, send_out = out_call(tab_b, d_attn, out, attended)
    half = FF // CHUNK // 2
    d_query, d_head0, dkv_low = attend_back_call(
        0, spot, query, kv_low, d_attended, stat, query_raw, cosine, sine, heads, ()
    )
    halo = shifted(dkv_low[:WINDOW].astype(bf16), -1)
    d_query, d_head1, dkv_high = attend_back_call(
        tokens - 2 * TILE, spot, query, kv, d_attended, stat, query_raw, cosine, sine, heads, (d_query,)
    )
    grad_in, keep_qkv, send_qkv = qkv_back_call(
        tab_b, hidden_in, gains, heads, d_query, dkv_high, dkv_low, halo, key_raw, cosine, sine, weight,
        d_mid, d_gains, d_head0, d_head1,
    )
    sum_ff, sum_down, sum_out = scatter_relative(
        [keep_ff, keep_down, keep_out], [send_ff, send_down, send_out], [route_a, route_a, route_b]
    )
    (sum_qkv,) = scatter_relative([keep_qkv], [send_qkv], [route_b])

    gate_up = sum_ff.reshape(FF // CHUNK, 2, 4, ROWS, LANES).transpose(1, 3, 0, 2, 4).reshape(2, -1)
    parts = sum_qkv[: 4 * ROWS].reshape(4, ROWS, GROUP).transpose(1, 0, 2).reshape(ROWS, QKV)
    summed = (
        parts[:, : NH * HD].reshape(-1),
        parts[:, NH * HD : NH * HD + HD].reshape(-1),
        parts[:, NH * HD + HD :].reshape(-1),
        sum_out.reshape(-1),
        gate_up[0],
        gate_up[1],
        sum_down.reshape(-1),
        sum_qkv[4 * ROWS, : s_gain.shape[0]],
    )
    if near > 1:
        summed = tuple(
            lax.psum_scatter(one, "flat", scatter_dimension=0, tiled=True, axis_index_groups=groups)
            for one in summed
        )
    return (output, grad_in) + tuple(summed)


def solution(mesh):
    rows = P("flat", None)
    flat = P("flat")
    return jax.shard_map(
        per_device,
        mesh=mesh,
        in_specs=(rows,) + (flat,) * 9 + (rows,),
        out_specs=(rows, rows) + (flat,) * 8,
        check_vma=False,
    )
```

```python
import functools

import jax
import jax.numpy as jnp
from jax import lax
from jax.experimental import pallas as pl
from jax.experimental.pallas import tpu as pltpu
from jax.sharding import PartitionSpec as P

D = 640
NH = 4
HD = 256
FF = 2048
WINDOW = 512

PIECES = 32
ROWS = D // PIECES
TILE = 256
QKV = (NH + 2) * HD
GROUP = QKV // 4
CHUNK = 512
LANES = 128
HALF = HD // 2
SCALE = HD ** (-0.5)

epsilon = 1e-06
rope_base = 10000.0

bf16 = jnp.bfloat16
f32 = jnp.float32


def params(megabytes):
    return pltpu.CompilerParams(vmem_limit_bytes=megabytes << 20)


def whole(shape, space=None):
    return pl.BlockSpec(shape, lambda i, *_: (0,) * len(shape))


def rows_of(width, first=0):
    return pl.BlockSpec((TILE, width), lambda i, *_: (i + first, 0))


def shifted(block, distance):
    devices = range(lax.axis_size("flat"))
    route = [(i - distance, i) for i in devices if i - distance in devices]
    return lax.ppermute(block, "flat", route)


def swapped(block, mask):
    count = lax.axis_size("flat")
    near = count // PIECES
    route = [(i, ((i // near) ^ mask) * near + i % near) for i in range(count)]
    return lax.ppermute(block, "flat", route)


def after(value, *others):
    return lax.optimization_barrier((value,) + others)[0]


def spread(held, masks):
    return jnp.concatenate([held] + [swapped(held, mask) for mask in masks])


def collected(total, masks):
    size = total.shape[0] // (len(masks) + 1)
    came = [
        swapped(total[size * (i + 1) : size * (i + 2)].astype(bf16), mask) for i, mask in enumerate(masks)
    ]
    own = total[:size].astype(f32)
    for one in came:
        own = own + one.astype(f32)
    return own


def chip_table(me, order):
    differ = (me >> 1) ^ jnp.arange(PIECES // 2, dtype=jnp.int32)
    place = jnp.zeros((PIECES // 2,), jnp.int32)
    for step, mask in enumerate(order):
        place = place + jnp.where((differ & (mask >> 1)) != 0, 1 << step, 0)
    return jnp.concatenate([place, (me & 1)[None]]).astype(jnp.int32)


def halved(held, routes, step):
    half = 1 << (3 - step)
    nxt = []
    for (keep, other), route in zip(held, routes):
        away = (keep[half:].astype(f32) + other[half:].astype(f32)).astype(bf16)
        stay = (keep[:half].astype(f32) + other[:half].astype(f32)).astype(bf16)
        nxt.append((stay, away, route[step]))
    return nxt


def sent(halves, *beside):
    return [(stay, after(swapped(away, mask), *beside)) for stay, away, mask in halves]


def settled(held):
    return [(keep.astype(f32) + other.astype(f32))[0] for keep, other in held]


def dot(left, right):
    return lax.dot_general(left, right, (((1,), (0,)), ((), ())), preferred_element_type=f32)


def dot_bt(left, right):
    return lax.dot_general(left, right, (((1,), (1,)), ((), ())), preferred_element_type=f32)


def dot_at(left, right):
    return lax.dot_general(left, right, (((0,), (0,)), ((), ())), preferred_element_type=f32)


def inv_rms(values):
    return lax.rsqrt(jnp.mean(values * values, axis=-1, keepdims=True) + epsilon)


def rms_back(values, inverse, gain, grad):
    scaled = grad * gain
    mean = jnp.mean(scaled * values, axis=-1, keepdims=True)
    return inverse * scaled - values * (inverse * inverse * inverse * mean)


def store_pair(keep, send, index, core, even, odd):
    mine, theirs = pair_of(core, even, odd)
    keep[index] = mine.astype(bf16)
    send[index] = theirs.astype(bf16)


def pair_of(core, own, other):
    mine = core == 0
    return jnp.where(mine, own, other), jnp.where(mine, other, own)


def qkv_kernel(
    tab_ref, hidden_ref, gain_ref, head_ref, own_ref, other_ref, cos_ref, sin_ref,
    query_ref, kv_ref, query_raw_ref, key_raw_ref, weight_ref,
):
    @pl.when(pl.program_id(0) == 0)
    def _():
        core = tab_ref[PIECES // 2]
        for e in range(PIECES // 2):
            for d, block in zip((2 * e, 2 * e + 1), pair_of(core, own_ref[tab_ref[e]], other_ref[tab_ref[e]])):
                for h in range(4):
                    weight_ref[ROWS * d : ROWS * (d + 1), GROUP * h : GROUP * (h + 1)] = block[
                        ROWS * h : ROWS * (h + 1)
                    ]

    inputs = hidden_ref[...].astype(f32)
    normed = (inputs * inv_rms(inputs) * gain_ref[0:1]).astype(bf16)
    raw = dot(normed, weight_ref[...])
    cosine = cos_ref[...]
    sine = sin_ref[...]

    def turned(values, gain):
        values = values * inv_rms(values) * gain
        first, second = values[:, :HALF], values[:, HALF:]
        return jnp.concatenate(
            [first * cosine - second * sine, second * cosine + first * sine], axis=1
        )

    for h in range(NH):
        columns = slice(HD * h, HD * (h + 1))
        query_ref[:, columns] = (turned(raw[:, columns], head_ref[0:1]) * SCALE).astype(bf16)
    query_raw_ref[...] = raw[:, : NH * HD]
    key_raw = raw[:, NH * HD : NH * HD + HD]
    key_raw_ref[...] = key_raw
    kv_ref[:, :HD] = turned(key_raw, head_ref[1:2]).astype(bf16)
    kv_ref[:, HD:] = raw[:, NH * HD + HD :].astype(bf16)


def qkv_call(tab, hidden, gains, heads, pieces, cosine, sine):
    tokens = hidden.shape[0]
    return pl.pallas_call(
        qkv_kernel,
        grid_spec=pltpu.PrefetchScalarGridSpec(
            num_scalar_prefetch=1,
            grid=(tokens // TILE,),
            in_specs=[
                rows_of(D), whole((8, D)), whole((8, HD)), *[whole(one.shape) for one in pieces],
                rows_of(HALF), rows_of(HALF),
            ],
            out_specs=[
                rows_of(NH * HD), rows_of(2 * HD), rows_of(NH * HD), rows_of(HD),
                whole((D, QKV)),
            ],
        ),
        out_shape=[
            jax.ShapeDtypeStruct((tokens, NH * HD), bf16),
            jax.ShapeDtypeStruct((tokens, 2 * HD), bf16),
            jax.ShapeDtypeStruct((tokens, NH * HD), f32),
            jax.ShapeDtypeStruct((tokens, HD), f32),
            jax.ShapeDtypeStruct((D, QKV), bf16),
        ],
        compiler_params=params(48),
        cost_estimate=pl.CostEstimate(flops=9 * 10**9, bytes_accessed=20 << 20, transcendentals=0),
        name="qkv",
    )(tab, hidden, gains, heads, *pieces, cosine, sine)


def allowed_keys(spot_ref, first):
    token = lax.broadcasted_iota(jnp.int32, (1, TILE), 1)
    spot = token + first
    position = jnp.where(spot < spot_ref[0], spot + spot_ref[1], spot - spot_ref[0])
    lowest = token + WINDOW - jnp.minimum(position, WINDOW - 1)
    key = lax.broadcasted_iota(jnp.int32, (TILE + WINDOW, TILE), 0)
    return (key >= lowest) & (key <= token + WINDOW)


def attend_kernel(start, unpacks, spot_ref, tab_ref, query_ref, kv_ref, *refs):
    step = pl.program_id(0)
    if unpacks:
        own_ref, other_ref, attended_ref, attn_ref, stat_ref, out_ref = refs

        @pl.when(step == 0)
        def _():
            for e in range(PIECES // 2):
                place = tab_ref[e]
                even, odd = pair_of(tab_ref[PIECES // 2], own_ref[place], other_ref[place])
                out_ref[64 * e : 64 * e + 32] = even
                out_ref[64 * e + 32 : 64 * (e + 1)] = odd
    else:
        out_ref = refs[0]
        attended_ref, attn_ref, stat_ref = refs[-3:]
    keys = kv_ref[pl.ds(step * TILE, TILE + WINDOW), :HD]
    values = kv_ref[pl.ds(step * TILE, TILE + WINDOW), HD:]
    values_t = values.T
    allowed = allowed_keys(spot_ref, start + step * TILE)
    for h in range(NH):
        columns = slice(HD * h, HD * (h + 1))
        scores = dot_bt(keys, query_ref[:, columns])
        expo = jnp.where(allowed, jnp.exp(scores), 0.0)
        total = jnp.sum(expo, axis=0, keepdims=True)
        mixed = dot(values_t, expo.astype(bf16)) * (1.0 / total)
        attended_ref[:, columns] = mixed.T.astype(bf16)
        stat_ref[h : h + 1, :] = jnp.log(total)
    attn_ref[...] = dot(attended_ref[...], out_ref[...])


def attend_call(start, spot, tab, query, kv, pieces, kept):
    tokens = query.shape[0]
    first = start // TILE
    unpacks = not kept
    outs = [
        jax.ShapeDtypeStruct((tokens, NH * HD), bf16),
        jax.ShapeDtypeStruct((tokens, D), f32),
        jax.ShapeDtypeStruct((8, tokens), f32),
    ]
    out_specs = [
        rows_of(NH * HD, first),
        rows_of(D, first),
        pl.BlockSpec((8, TILE), lambda i, *_: (0, i + first)),
    ]
    if unpacks:
        outs.append(jax.ShapeDtypeStruct((NH * HD, D), bf16))
        out_specs.append(whole((NH * HD, D)))
    return pl.pallas_call(
        functools.partial(attend_kernel, start, unpacks),
        grid_spec=pltpu.PrefetchScalarGridSpec(
            num_scalar_prefetch=2,
            grid=(2,),
            in_specs=[rows_of(NH * HD, first), whole(kv.shape)]
            + [whole(one.shape) for one in pieces]
            + [pl.BlockSpec(memory_space=pl.ANY)] * len(kept),
            out_specs=out_specs,
        ),
        out_shape=outs,
        input_output_aliases={4 + len(pieces) + i: i for i in range(len(kept))},
        compiler_params=params(48),
        cost_estimate=pl.CostEstimate(flops=7 * 10**9, bytes_accessed=8 << 20, transcendentals=1 << 21),
        name="attend",
    )(spot, tab, query, kv, *pieces, *kept)


def ffn_kernel(
    tab_ref, tab_back_ref, tab_down_ref, hidden_ref, attn_ref, cot_ref, gain_ref,
    packed_ref, down_ref,
    output_ref, dmid_ref, dattn_ref, dgain_ref, gate_keep_ref, gate_send_ref, up_keep_ref, up_send_ref,
    down_keep_ref, down_send_ref,
    middle_ref, normed_ref, normed_t_ref, sum_ref, dffn_ref, gate_w, up_w, down_w, inner_ref, slope_ref, act_ref,
):
    step = pl.program_id(0)
    tokens = hidden_ref.shape[0]
    parts = tokens // TILE
    chunks = FF // CHUNK
    core = tab_ref[PIECES // 2]

    @pl.when(step == 0)
    def _():
        def one(part, _):
            rows = pl.ds(pl.multiple_of(part * TILE, TILE), TILE)
            branch = attn_ref[rows]
            middle = hidden_ref[rows].astype(f32) + branch * inv_rms(branch) * gain_ref[1:2]
            middle_ref[rows] = middle
            normed_ref[rows] = (middle * inv_rms(middle) * gain_ref[2:3]).astype(bf16)
            return 0

        lax.fori_loop(0, parts, one, 0)
        normed_t_ref[...] = normed_ref[...].T

    @pl.when(step < chunks)
    def _():
        for d in range(PIECES):
            for j in range(CHUNK // LANES):
                columns = slice(LANES * j, LANES * (j + 1))
                rows = slice(ROWS * d, ROWS * (d + 1))
                gate_w[step, rows, columns] = packed_ref[d, ROWS * j : ROWS * (j + 1)]
                up_w[step, rows, columns] = packed_ref[d, 80 + ROWS * j : 80 + ROWS * (j + 1)]
        for i in range(CHUNK // 64):
            for g in range(D // LANES):
                down_w[step, 64 * i : 64 * (i + 1), LANES * g : LANES * (g + 1)] = down_ref[
                    i, 64 * g : 64 * (g + 1)
                ]
        for part in range(parts):
            rows = slice(part * TILE, (part + 1) * TILE)
            gate = dot(normed_ref[rows], gate_w[step])
            upward = dot(normed_ref[rows], up_w[step])
            square = gate * gate
            c0 = 0.7978845608028654
            c1 = c0 * 0.044715
            half = 0.5 * jnp.tanh(gate * (c0 + c1 * square)) + 0.5
            active = gate * half
            slope = half + 2.0 * active * (1.0 - half) * (c0 + 3.0 * c1 * square)
            inner = (active * upward).astype(bf16)
            inner_ref[step, rows] = inner
            act_ref[step, rows] = active.astype(bf16)
            slope_ref[step, rows] = (slope * upward).astype(bf16)
            more = dot(inner, down_w[step])

            @pl.when(step == 0)
            def _():
                sum_ref[rows] = more

            @pl.when(step > 0)
            def _():
                sum_ref[rows] += more

    @pl.when(step == chunks - 1)
    def _():
        def one(part, total):
            rows = pl.ds(pl.multiple_of(part * TILE, TILE), TILE)
            branch = sum_ref[rows]
            inverse = inv_rms(branch)
            grad = cot_ref[rows].astype(f32)
            output_ref[rows] = (middle_ref[rows] + branch * inverse * gain_ref[3:4]).astype(bf16)
            dffn_ref[rows] = rms_back(branch, inverse, gain_ref[3:4], grad).astype(bf16)
            return total + jnp.sum(grad * branch * inverse, axis=0, keepdims=True)

        dgain_ref[...] = jnp.zeros_like(dgain_ref)
        dgain_ref[3:4] = lax.fori_loop(0, parts, one, jnp.zeros((1, D), f32))

    @pl.when(step >= chunks)
    def _():
        chunk = step - chunks
        d_inner = dot_bt(dffn_ref[...], down_w[chunk])
        d_gate = (d_inner * slope_ref[chunk].astype(f32)).astype(bf16)
        d_up = (d_inner * act_ref[chunk].astype(f32)).astype(bf16)
        more = dot_bt(d_gate, gate_w[chunk]) + dot_bt(d_up, up_w[chunk])

        @pl.when(chunk == 0)
        def _():
            sum_ref[...] = more

        @pl.when(chunk > 0)
        def _():
            sum_ref[...] += more

        for grad_in, place_ref, keep_ref, send_ref in (
            (d_gate, tab_ref, gate_keep_ref, gate_send_ref), (d_up, tab_back_ref, up_keep_ref, up_send_ref),
        ):
            for j in range(CHUNK // LANES // 2):
                grad = dot(normed_t_ref[...], grad_in[:, 256 * j : 256 * (j + 1)])
                for k in range(2):
                    low = ROWS * (2 * j + k)
                    for e in range(PIECES // 2):
                        even = grad[2 * ROWS * e : 2 * ROWS * e + ROWS, LANES * k : LANES * (k + 1)]
                        odd = grad[2 * ROWS * e + ROWS : 2 * ROWS * (e + 1), LANES * k : LANES * (k + 1)]
                        even, odd = pair_of(core, even, odd)
                        keep_ref[place_ref[e], 0, low : low + ROWS] = even.astype(bf16)
                        send_ref[place_ref[e], 0, low : low + ROWS] = odd.astype(bf16)
        grad = dot_at(inner_ref[chunk], dffn_ref[...])
        for i in range(CHUNK // 128):
            place = tab_down_ref[chunk * (CHUNK // 128) + i]
            store_pair(
                down_keep_ref, down_send_ref, place, core,
                grad[128 * i : 128 * i + 64], grad[128 * i + 64 : 128 * (i + 1)],
            )

    @pl.when(step == 2 * chunks - 1)
    def _():
        def one(part, totals):
            rows = pl.ds(pl.multiple_of(part * TILE, TILE), TILE)
            middle = middle_ref[rows]
            inverse = inv_rms(middle)
            grad = sum_ref[rows]
            d_mid = cot_ref[rows].astype(f32) + rms_back(middle, inverse, gain_ref[2:3], grad)
            pre = jnp.sum(grad * middle * inverse, axis=0, keepdims=True)
            branch = attn_ref[rows]
            inverse = inv_rms(branch)
            dmid_ref[rows] = d_mid
            dattn_ref[rows] = rms_back(branch, inverse, gain_ref[1:2], d_mid).astype(bf16)
            mid = jnp.sum(d_mid * branch * inverse, axis=0, keepdims=True)
            return totals[0] + mid, totals[1] + pre

        zero = jnp.zeros((1, D), f32)
        mid, pre = lax.fori_loop(0, parts, one, (zero, zero))
        dgain_ref[1:2] = mid
        dgain_ref[2:3] = pre


def ffn_call(tabs, hidden, attn_out, cotangent, gains, packed):
    tokens = hidden.shape[0]
    chunks = FF // CHUNK
    pairs = PIECES // 2
    once = pl.Buffered(1)

    def single(shape):
        return pl.BlockSpec(shape, lambda i, *_: (0,) * len(shape), pipeline_mode=once)

    return pl.pallas_call(
        ffn_kernel,
        grid_spec=pltpu.PrefetchScalarGridSpec(
            num_scalar_prefetch=len(tabs),
            grid=(2 * chunks,),
            in_specs=[
                single((tokens, D)), single((tokens, D)), single((tokens, D)), whole((8, D)),
                pl.BlockSpec((PIECES, 160, LANES), lambda i, *_: (0, jnp.minimum(i, chunks - 1), 0)),
                pl.BlockSpec((8, 320, LANES), lambda i, *_: (jnp.minimum(i, chunks - 1), 2, 0)),
            ],
            out_specs=[
                single((tokens, D)), single((tokens, D)), single((tokens, D)), whole((8, D)),
                *[pl.BlockSpec((pairs, 1, 80, LANES), lambda i, *_: (0, jnp.maximum(i - chunks, 0), 0, 0))] * 4,
                single((pairs, 64, D)), single((pairs, 64, D)),
            ],
            scratch_shapes=[
                pltpu.VMEM((tokens, D), f32),
                pltpu.VMEM((tokens, D), bf16),
                pltpu.VMEM((D, tokens), bf16),
                pltpu.VMEM((tokens, D), f32),
                pltpu.VMEM((tokens, D), bf16),
                pltpu.VMEM((chunks, D, CHUNK), bf16),
                pltpu.VMEM((chunks, D, CHUNK), bf16),
                pltpu.VMEM((chunks, CHUNK, D), bf16),
                pltpu.VMEM((chunks, tokens, CHUNK), bf16),
                pltpu.VMEM((chunks, tokens, CHUNK), bf16),
                pltpu.VMEM((chunks, tokens, CHUNK), bf16),
            ],
        ),
        out_shape=[
            jax.ShapeDtypeStruct((tokens, D), bf16),
            jax.ShapeDtypeStruct((tokens, D), f32),
            jax.ShapeDtypeStruct((tokens, D), bf16),
            jax.ShapeDtypeStruct((8, D), f32),
            *[jax.ShapeDtypeStruct((pairs, chunks, 80, LANES), bf16)] * 4,
            jax.ShapeDtypeStruct((pairs, 64, D), bf16),
            jax.ShapeDtypeStruct((pairs, 64, D), bf16),
        ],
        compiler_params=params(60),
        cost_estimate=pl.CostEstimate(flops=60 * 10**9, bytes_accessed=30 << 20, transcendentals=tokens * FF),
        name="feed_forward",
    )(*tabs, hidden, attn_out, cotangent, gains, packed, packed)


def out_kernel(tab_ref, dattn_ref, out_ref, attended_ref, datt_ref, keep_ref, send_ref):
    core = tab_ref[PIECES // 2]
    datt_ref[...] = dot_bt(dattn_ref[...], out_ref[...]).astype(bf16)
    for b in range(NH * HD // 256):
        grad = dot_at(attended_ref[:, 256 * b : 256 * (b + 1)], dattn_ref[...])
        for i in range(4):
            store_pair(
                keep_ref, send_ref, tab_ref[4 * b + i], core,
                grad[64 * i : 64 * i + 32], grad[64 * i + 32 : 64 * (i + 1)],
            )


def out_call(tab, d_attn, out, attended):
    tokens = d_attn.shape[0]
    pairs = PIECES // 2
    return pl.pallas_call(
        out_kernel,
        grid_spec=pltpu.PrefetchScalarGridSpec(
            num_scalar_prefetch=1,
            grid=(1,),
            in_specs=[whole(d_attn.shape), whole(out.shape), whole(attended.shape)],
            out_specs=[whole((tokens, NH * HD)), whole((pairs, 32, D)), whole((pairs, 32, D))],
        ),
        out_shape=[
            jax.ShapeDtypeStruct((tokens, NH * HD), bf16),
            jax.ShapeDtypeStruct((pairs, 32, D), bf16),
            jax.ShapeDtypeStruct((pairs, 32, D), bf16),
        ],
        compiler_params=params(48),
        cost_estimate=pl.CostEstimate(flops=6 * 10**9, bytes_accessed=8 << 20, transcendentals=0),
        name="out_backward",
    )(tab, d_attn, out, attended)


def attend_back_kernel(
    start, spot_ref, query_ref, kv_ref, datt_ref, stat_ref, raw_ref, cos_ref, sin_ref, head_ref, *refs
):
    dquery_ref, dgain_ref, dkv_ref = refs[-3:]
    step = pl.program_id(0)

    @pl.when(step == 0)
    def _():
        dkv_ref[...] = jnp.zeros_like(dkv_ref)
        dgain_ref[...] = jnp.zeros_like(dgain_ref)

    span = pl.ds(step * TILE, TILE + WINDOW)
    keys = kv_ref[span, :HD]
    values = kv_ref[span, HD:]
    keys_t = keys.T
    allowed = allowed_keys(spot_ref, start + step * TILE)
    cosine = cos_ref[...]
    sine = sin_ref[...]
    gain = head_ref[0:1]
    d_gain = jnp.zeros((1, HD), f32)
    for h in range(NH):
        columns = slice(HD * h, HD * (h + 1))
        query = query_ref[:, columns]
        grad = datt_ref[:, columns]
        scores = dot_bt(keys, query) - stat_ref[h : h + 1, :]
        probs = jnp.where(allowed, jnp.exp(scores), 0.0)
        d_probs = dot_bt(values, grad)
        inside = jnp.sum(probs * d_probs, axis=0, keepdims=True)
        d_scores = (probs * (d_probs - inside)).astype(bf16)
        dkv_ref[span, HD:] += dot(probs.astype(bf16), grad)
        dkv_ref[span, :HD] += dot(d_scores, query)
        turned = dot(keys_t, d_scores).T * SCALE
        first, second = turned[:, :HALF], turned[:, HALF:]
        turned = jnp.concatenate(
            [first * cosine + second * sine, second * cosine - first * sine], axis=1
        )
        raw = raw_ref[:, columns]
        inverse = inv_rms(raw)
        dquery_ref[:, columns] = rms_back(raw, inverse, gain, turned).astype(bf16)
        d_gain = d_gain + jnp.sum(turned * raw * inverse, axis=0, keepdims=True)
    dgain_ref[0:1] += d_gain


def attend_back_call(start, spot, query, kv, d_attended, stat, query_raw, cosine, sine, heads, kept):
    tokens = query.shape[0]
    first = start // TILE
    return pl.pallas_call(
        functools.partial(attend_back_kernel, start),
        grid_spec=pltpu.PrefetchScalarGridSpec(
            num_scalar_prefetch=1,
            grid=(2,),
            in_specs=[
                rows_of(NH * HD, first), whole(kv.shape), rows_of(NH * HD, first),
                pl.BlockSpec((8, TILE), lambda i, *_: (0, i + first)),
                rows_of(NH * HD, first), rows_of(HALF, first), rows_of(HALF, first), whole((8, HD)),
            ]
            + [pl.BlockSpec(memory_space=pl.ANY)] * len(kept),
            out_specs=[rows_of(NH * HD, first), whole((8, HD)), whole(kv.shape)],
        ),
        out_shape=[
            jax.ShapeDtypeStruct((tokens, NH * HD), bf16),
            jax.ShapeDtypeStruct((8, HD), f32),
            jax.ShapeDtypeStruct(kv.shape, f32),
        ],
        input_output_aliases={9 + i: i for i in range(len(kept))},
        compiler_params=params(48),
        cost_estimate=pl.CostEstimate(flops=12 * 10**9, bytes_accessed=10 << 20, transcendentals=1 << 21),
        name="attend_backward",
    )(spot, query, kv, d_attended, stat, query_raw, cosine, sine, heads, *kept)


def qkv_back_kernel(
    tab_ref, hidden_ref, gain_ref, head_ref, dquery_ref, near_ref, early_ref, halo_ref, key_raw_ref,
    cos_ref, sin_ref, weight_ref, dmid_ref, dffn_gain_ref, dhead0_ref, dhead1_ref,
    grad_ref, keep_ref, send_ref, normed_ref, dqkv_ref, din_ref, dkey_ref,
):
    step = pl.program_id(0)
    rows = pl.ds(pl.multiple_of(step * TILE, TILE), TILE)
    core = tab_ref[PIECES // 2]

    @pl.when(step == 0)
    def _():
        din_ref[...] = jnp.zeros_like(din_ref)
        dkey_ref[...] = jnp.zeros_like(dkey_ref)

    inputs = hidden_ref[...].astype(f32)
    inverse = inv_rms(inputs)
    normed_ref[rows] = (inputs * inverse * gain_ref[0:1]).astype(bf16)
    d_kv = near_ref[...] + jnp.where(step < 2, early_ref[...], halo_ref[...].astype(f32))
    cosine = cos_ref[...]
    sine = sin_ref[...]
    first, second = d_kv[:, :HALF], d_kv[:, HALF:HD]
    turned = jnp.concatenate(
        [first * cosine + second * sine, second * cosine - first * sine], axis=1
    )
    raw = key_raw_ref[...]
    raw_inverse = inv_rms(raw)
    dkey_ref[0:1] += jnp.sum(turned * raw * raw_inverse, axis=0, keepdims=True)
    dqkv_ref[rows, : NH * HD] = dquery_ref[...]
    dqkv_ref[rows, NH * HD : NH * HD + HD] = rms_back(raw, raw_inverse, head_ref[1:2], turned).astype(bf16)
    dqkv_ref[rows, NH * HD + HD :] = d_kv[:, HD:].astype(bf16)
    d_normed = dot_bt(dqkv_ref[rows], weight_ref[...])
    din_ref[0:1] += jnp.sum(d_normed * inputs * inverse, axis=0, keepdims=True)
    grad_ref[...] = (dmid_ref[...] + rms_back(inputs, inverse, gain_ref[0:1], d_normed)).astype(bf16)

    @pl.when(step == pl.num_programs(0) - 1)
    def _():
        for h in range(4):
            rows_h = slice(ROWS * h, ROWS * (h + 1))
            grad = dot_at(normed_ref[...], dqkv_ref[:, GROUP * h : GROUP * (h + 1)])
            for e in range(PIECES // 2):
                even = grad[2 * ROWS * e : 2 * ROWS * e + ROWS]
                odd = grad[2 * ROWS * e + ROWS : 2 * ROWS * (e + 1)]
                place = tab_ref[e]
                mine, theirs = pair_of(core, even, odd)
                keep_ref[place, rows_h] = mine.astype(bf16)
                send_ref[place, rows_h] = theirs.astype(bf16)
        gains = jnp.concatenate(
            [
                din_ref[0:1], dffn_gain_ref[1:2], dffn_gain_ref[2:3], dffn_gain_ref[3:4],
                dhead0_ref[0:1] + dhead1_ref[0:1], dkey_ref[0:1],
            ],
            axis=1,
        )
        piece = gains.shape[1] // PIECES
        for e in range(PIECES // 2):
            even = jnp.broadcast_to(gains[:, 2 * piece * e : 2 * piece * e + piece], (8, piece))
            odd = jnp.broadcast_to(gains[:, 2 * piece * e + piece : 2 * piece * (e + 1)], (8, piece))
            place = tab_ref[e]
            keep_ref[place, 80:88] = jnp.zeros((8, GROUP), bf16)
            send_ref[place, 80:88] = jnp.zeros((8, GROUP), bf16)
            even, odd = pair_of(core, even, odd)
            keep_ref[place, 80:88, 0:piece] = even.astype(bf16)
            send_ref[place, 80:88, 0:piece] = odd.astype(bf16)


def qkv_back_call(
    tab, hidden, gains, heads, d_query, near, early, halo, key_raw, cosine, sine, weight, d_mid,
    d_gains, d_head0, d_head1,
):
    tokens = hidden.shape[0]
    pairs = PIECES // 2
    last = WINDOW // TILE
    return pl.pallas_call(
        qkv_back_kernel,
        grid_spec=pltpu.PrefetchScalarGridSpec(
            num_scalar_prefetch=1,
            grid=(tokens // TILE,),
            in_specs=[
                rows_of(D), whole((8, D)), whole((8, HD)), rows_of(NH * HD), rows_of(2 * HD),
                pl.BlockSpec((TILE, 2 * HD), lambda i, *_: (jnp.minimum(i + last, 2 * last - 1), 0)),
                pl.BlockSpec((TILE, 2 * HD), lambda i, *_: (jnp.clip(i - last, 0, last - 1), 0)),
                rows_of(HD), rows_of(HALF), rows_of(HALF), whole((D, QKV)), rows_of(D),
                whole((8, D)), whole((8, HD)), whole((8, HD)),
            ],
            out_specs=[rows_of(D), whole((pairs, 88, GROUP)), whole((pairs, 88, GROUP))],
            scratch_shapes=[
                pltpu.VMEM((tokens, D), bf16),
                pltpu.VMEM((tokens, QKV), bf16),
                pltpu.VMEM((8, D), f32),
                pltpu.VMEM((8, HD), f32),
            ],
        ),
        out_shape=[
            jax.ShapeDtypeStruct((tokens, D), bf16),
            jax.ShapeDtypeStruct((pairs, 88, GROUP), bf16),
            jax.ShapeDtypeStruct((pairs, 88, GROUP), bf16),
        ],
        compiler_params=params(48),
        cost_estimate=pl.CostEstimate(flops=13 * 10**9, bytes_accessed=16 << 20, transcendentals=0),
        name="qkv_backward",
    )(
        tab, hidden, gains, heads, d_query, near, early, halo, key_raw, cosine, sine, weight, d_mid,
        d_gains, d_head0, d_head1,
    )


def rotary_tables(positions):
    inverse = rope_base ** (-(jnp.arange(HALF, dtype=f32) * 2.0 / HD))
    angles = positions.astype(f32)[:, None] * inverse[None, :]
    return (jnp.cos(angles), jnp.sin(angles))


def per_device(
    hidden_in, segments, w_query, w_key, w_value, w_out, w_gate, w_up, w_down, norm_gains, cotangent
):
    tokens = hidden_in.shape[0]
    count = lax.axis_size("flat")
    near = count // PIECES
    me = lax.axis_index("flat") // near
    groups = [[p * near + i for i in range(near)] for p in range(PIECES)]
    shards = (w_query, w_key, w_value, w_out, w_gate, w_up, w_down, norm_gains)
    if near > 1:
        shards = [
            lax.all_gather(one, "flat", axis=0, tiled=True, axis_index_groups=groups) for one in shards
        ]
    s_query, s_key, s_value, s_out, s_gate, s_up, s_down, s_gain = shards

    gate_up = jnp.stack([s_gate.reshape(ROWS, -1, 4, LANES), s_up.reshape(ROWS, -1, 4, LANES)], axis=2)
    gate_up = gate_up.transpose(1, 2, 3, 0, 4).reshape(-1, LANES)
    down = s_down.reshape(-1, D // LANES, LANES).transpose(1, 0, 2).reshape(-1, LANES)
    columns = [[p * near + i for p in range(PIECES)] for i in range(near)]
    ffn_packed = lax.all_gather(
        jnp.concatenate([gate_up, down]), "flat", axis=0, tiled=False,
        axis_index_groups=columns if near > 1 else None,
    )

    qkv = jnp.concatenate(
        [s_query.reshape(ROWS, -1), s_key.reshape(ROWS, -1), s_value.reshape(ROWS, -1)], axis=1
    )
    gain_row = jnp.pad(s_gain[None], ((0, 7), (0, GROUP - s_gain.shape[0])))
    qkv = jnp.concatenate([qkv[:, GROUP * h : GROUP * (h + 1)] for h in range(4)] + [gain_row])
    over_z = (8, 16, 24)
    over_plane = (2, 4, 6)
    tab = chip_table(me, (8, 16, 2, 4))
    held = spread(qkv[None], over_z)
    held_out = spread(after(s_out.reshape(-1, D)[None], held), over_z)
    held = spread(held, over_plane)
    qkv_packed = (held, swapped(held, 1))
    held_out = spread(after(held_out, held), over_plane)
    pieces = jnp.stack([one[:, 80, : s_gain.shape[0]] for one in qkv_packed], axis=1)
    pieces = jnp.where((me & 1) == 0, pieces, pieces[:, ::-1])
    gain_all = jnp.take(pieces, tab[: PIECES // 2], axis=0).astype(f32).reshape(-1)
    gains = jnp.pad(gain_all[: 4 * D].reshape(4, D), ((0, 4), (0, 0)))
    heads = jnp.pad(gain_all[4 * D :].reshape(2, HD), ((0, 6), (0, 0)))

    rise = jnp.sum((segments == segments[0]).astype(jnp.int32))
    told = shifted(jnp.stack([segments[tokens - 1] + 1, tokens - rise]), 1)
    ahead = jnp.where(told[0] == segments[0] + 1, told[1], 0)
    index = jnp.arange(tokens, dtype=jnp.int32)
    positions = jnp.where(index < rise, index + ahead, index - rise)
    spot = jnp.stack([rise, ahead]).astype(jnp.int32)
    cosine, sine = rotary_tables(positions)

    query, kv, query_raw, key_raw, weight = qkv_call(
        tab, hidden_in, gains, heads, qkv_packed, cosine, sine
    )
    kv_prev = shifted(kv[tokens - WINDOW :], 1)
    held_out = after(held_out, query)
    *upper, out = attend_call(
        tokens - 2 * TILE, spot, tab, query, kv, (held_out, swapped(held_out, 1)), ()
    )
    kv_low = jnp.concatenate([kv_prev, kv[: tokens - WINDOW]])
    attended, attn_out, stat = attend_call(0, spot, tab, query, kv_low, (out,), upper)

    routes = ((2, 4, 8, 16), (4, 8, 2, 16), (8, 2, 4, 16))
    route_late = (4, 2, 8, 16)
    tabs = [chip_table(me, route[::-1]) for route in routes]
    tab_late = chip_table(me, route_late[::-1])
    output, d_mid, d_attn, d_gains, *pieces = ffn_call(
        tabs, hidden_in, attn_out, cotangent, gains, ffn_packed
    )
    held = [swapped(pieces[2 * i + 1], 1) for i in range(3)]
    d_attended, keep_out, send_out = out_call(tab_late, d_attn, out, attended)
    held = [(pieces[2 * i], after(held[i], d_attended)) for i in range(3)]
    halves = halved(held, routes, 0)
    d_query, d_head0, dkv_low = attend_back_call(
        0, spot, query, kv_low, after(d_attended, *[one[1] for one in halves]), stat, query_raw, cosine, sine,
        heads, (),
    )
    held = sent(halves, dkv_low)
    held_out = [(keep_out, after(swapped(send_out, 1), dkv_low))]
    halo = shifted(dkv_low[:WINDOW].astype(bf16), -1)
    halves = halved(held, routes, 1)
    halves_out = halved(held_out, (route_late,), 0)
    d_query, d_head1, dkv_high = attend_back_call(
        tokens - 2 * TILE, spot, query, kv, after(d_attended, *[one[1] for one in halves + halves_out]), stat,
        query_raw, cosine, sine, heads, (d_query,),
    )
    held = sent(halves, dkv_high)
    held_out = sent(halves_out, dkv_high)
    halves = halved(held, routes, 2)
    halves_out = halved(held_out, (route_late,), 1)
    grad_in, keep_qkv, send_qkv = qkv_back_call(
        tab, after(hidden_in, *[one[1] for one in halves + halves_out]), gains, heads, d_query, dkv_high,
        dkv_low, halo, key_raw, cosine, sine, weight, d_mid, d_gains, d_head0, d_head1,
    )
    held = sent(halves, keep_qkv)
    held_out = sent(halves_out, keep_qkv)
    total = keep_qkv.astype(f32) + swapped(send_qkv, 1).astype(f32)
    sum_qkv = collected(collected(total, over_plane), over_z)[0]
    held = sent(halved(held, routes, 3))
    sum_gate, sum_up, sum_down = settled(held)
    for step in range(2, 4):
        held_out = sent(halved(held_out, (route_late,), step))
    (sum_out,) = settled(held_out)

    gate_up = [one.reshape(-1, ROWS, LANES).transpose(1, 0, 2).reshape(-1) for one in (sum_gate, sum_up)]
    parts = sum_qkv[: 4 * ROWS].reshape(4, ROWS, GROUP).transpose(1, 0, 2).reshape(ROWS, QKV)
    summed = (
        parts[:, : NH * HD].reshape(-1),
        parts[:, NH * HD : NH * HD + HD].reshape(-1),
        parts[:, NH * HD + HD :].reshape(-1),
        sum_out.reshape(-1),
        gate_up[0],
        gate_up[1],
        sum_down.reshape(-1),
        sum_qkv[4 * ROWS, : s_gain.shape[0]],
    )
    if near > 1:
        summed = tuple(
            lax.psum_scatter(one, "flat", scatter_dimension=0, tiled=True, axis_index_groups=groups)
            for one in summed
        )
    return (output, grad_in) + tuple(summed)


def solution(mesh):
    rows = P("flat", None)
    flat = P("flat")
    return jax.shard_map(
        per_device,
        mesh=mesh,
        in_specs=(rows,) + (flat,) * 9 + (rows,),
        out_specs=(rows, rows) + (flat,) * 8,
        check_vma=False,
    )
```

```python
import functools

import jax
import jax.numpy as jnp
from jax import lax
from jax.experimental import pallas as pl
from jax.experimental.pallas import tpu as pltpu
from jax.sharding import PartitionSpec as P

D = 640
NH = 4
HD = 256
FF = 2048
WINDOW = 512

PIECES = 32
ROWS = D // PIECES
TILE = 256
QKV = (NH + 2) * HD
GROUP = QKV // 4
CHUNK = 512
LANES = 128
HALF = HD // 2
SCALE = HD ** (-0.5)

epsilon = 1e-06
rope_base = 10000.0

bf16 = jnp.bfloat16
f32 = jnp.float32


def params(megabytes):
    return pltpu.CompilerParams(vmem_limit_bytes=megabytes << 20)


def whole(shape, space=None):
    return pl.BlockSpec(shape, lambda i, *_: (0,) * len(shape))


def rows_of(width, first=0):
    return pl.BlockSpec((TILE, width), lambda i, *_: (i + first, 0))


def shifted(block, distance):
    devices = range(lax.axis_size("flat"))
    route = [(i - distance, i) for i in devices if i - distance in devices]
    return lax.ppermute(block, "flat", route)


def swapped(block, mask):
    count = lax.axis_size("flat")
    near = count // PIECES
    route = [(i, ((i // near) ^ mask) * near + i % near) for i in range(count)]
    return lax.ppermute(block, "flat", route)


def after(value, *others):
    return lax.optimization_barrier((value,) + others)[0]


def spread(held, masks):
    return jnp.concatenate([held] + [swapped(held, mask) for mask in masks])


def collected(total, masks):
    size = total.shape[0] // (len(masks) + 1)
    came = [
        swapped(total[size * (i + 1) : size * (i + 2)].astype(bf16), mask) for i, mask in enumerate(masks)
    ]
    own = total[:size].astype(f32)
    for one in came:
        own = own + one.astype(f32)
    return own


def chip_table(me, order):
    differ = (me >> 1) ^ jnp.arange(PIECES // 2, dtype=jnp.int32)
    place = jnp.zeros((PIECES // 2,), jnp.int32)
    for step, mask in enumerate(order):
        place = place + jnp.where((differ & (mask >> 1)) != 0, 1 << step, 0)
    return jnp.concatenate([place, (me & 1)[None]]).astype(jnp.int32)


def halved(held, routes, step):
    half = 1 << (3 - step)
    nxt = []
    for (keep, other), route in zip(held, routes):
        away = (keep[half:].astype(f32) + other[half:].astype(f32)).astype(bf16)
        stay = (keep[:half].astype(f32) + other[:half].astype(f32)).astype(bf16)
        nxt.append((stay, away, route[step]))
    return nxt


def sent(halves, *beside):
    return [(stay, after(swapped(away, mask), *beside)) for stay, away, mask in halves]


def settled(held):
    return [(keep.astype(f32) + other.astype(f32))[0] for keep, other in held]


def dot(left, right):
    return lax.dot_general(left, right, (((1,), (0,)), ((), ())), preferred_element_type=f32)


def dot_bt(left, right):
    return lax.dot_general(left, right, (((1,), (1,)), ((), ())), preferred_element_type=f32)


def dot_at(left, right):
    return lax.dot_general(left, right, (((0,), (0,)), ((), ())), preferred_element_type=f32)


def inv_rms(values):
    return lax.rsqrt(jnp.mean(values * values, axis=-1, keepdims=True) + epsilon)


def rms_back(values, inverse, gain, grad):
    scaled = grad * gain
    mean = jnp.mean(scaled * values, axis=-1, keepdims=True)
    return inverse * scaled - values * (inverse * inverse * inverse * mean)


def store_pair(keep, send, index, rows, core, even, odd):
    mine, theirs = pair_of(core, even, odd)
    keep[index, rows] = mine.astype(bf16)
    send[index, rows] = theirs.astype(bf16)


def pair_of(core, own, other):
    mine = core == 0
    return jnp.where(mine, own, other), jnp.where(mine, other, own)


def qkv_kernel(
    tab_ref, hidden_ref, gain_ref, head_ref, own_ref, other_ref, cos_ref, sin_ref,
    query_ref, kv_ref, query_raw_ref, key_raw_ref, weight_ref,
):
    @pl.when(pl.program_id(0) == 0)
    def _():
        core = tab_ref[PIECES // 2]
        for e in range(PIECES // 2):
            for d, block in zip((2 * e, 2 * e + 1), pair_of(core, own_ref[tab_ref[e]], other_ref[tab_ref[e]])):
                for h in range(4):
                    weight_ref[ROWS * d : ROWS * (d + 1), GROUP * h : GROUP * (h + 1)] = block[
                        ROWS * h : ROWS * (h + 1)
                    ]

    inputs = hidden_ref[...].astype(f32)
    normed = (inputs * inv_rms(inputs) * gain_ref[0:1]).astype(bf16)
    raw = dot(normed, weight_ref[...])
    cosine = cos_ref[...]
    sine = sin_ref[...]

    def turned(values, gain):
        values = values * inv_rms(values) * gain
        first, second = values[:, :HALF], values[:, HALF:]
        return jnp.concatenate(
            [first * cosine - second * sine, second * cosine + first * sine], axis=1
        )

    for h in range(NH):
        columns = slice(HD * h, HD * (h + 1))
        query_ref[:, columns] = (turned(raw[:, columns], head_ref[0:1]) * SCALE).astype(bf16)
    query_raw_ref[...] = raw[:, : NH * HD]
    key_raw = raw[:, NH * HD : NH * HD + HD]
    key_raw_ref[...] = key_raw
    kv_ref[:, :HD] = turned(key_raw, head_ref[1:2]).astype(bf16)
    kv_ref[:, HD:] = raw[:, NH * HD + HD :].astype(bf16)


def qkv_call(tab, hidden, gains, heads, pieces, cosine, sine):
    tokens = hidden.shape[0]
    return pl.pallas_call(
        qkv_kernel,
        grid_spec=pltpu.PrefetchScalarGridSpec(
            num_scalar_prefetch=1,
            grid=(tokens // TILE,),
            in_specs=[
                rows_of(D), whole((8, D)), whole((8, HD)), *[whole(one.shape) for one in pieces],
                rows_of(HALF), rows_of(HALF),
            ],
            out_specs=[
                rows_of(NH * HD), rows_of(2 * HD), rows_of(NH * HD), rows_of(HD),
                whole((D, QKV)),
            ],
        ),
        out_shape=[
            jax.ShapeDtypeStruct((tokens, NH * HD), bf16),
            jax.ShapeDtypeStruct((tokens, 2 * HD), bf16),
            jax.ShapeDtypeStruct((tokens, NH * HD), f32),
            jax.ShapeDtypeStruct((tokens, HD), f32),
            jax.ShapeDtypeStruct((D, QKV), bf16),
        ],
        compiler_params=params(48),
        cost_estimate=pl.CostEstimate(flops=9 * 10**9, bytes_accessed=20 << 20, transcendentals=0),
        name="qkv",
    )(tab, hidden, gains, heads, *pieces, cosine, sine)


def allowed_keys(spot_ref, first):
    token = lax.broadcasted_iota(jnp.int32, (1, TILE), 1)
    spot = token + first
    position = jnp.where(spot < spot_ref[0], spot + spot_ref[1], spot - spot_ref[0])
    lowest = token + WINDOW - jnp.minimum(position, WINDOW - 1)
    key = lax.broadcasted_iota(jnp.int32, (TILE + WINDOW, TILE), 0)
    return (key >= lowest) & (key <= token + WINDOW)


def attend_kernel(start, unpacks, spot_ref, tab_ref, query_ref, kv_ref, *refs):
    step = pl.program_id(0)
    if unpacks:
        own_ref, other_ref, attended_ref, attn_ref, stat_ref, out_ref = refs

        @pl.when(step == 0)
        def _():
            for e in range(PIECES // 2):
                place = tab_ref[e]
                even, odd = pair_of(tab_ref[PIECES // 2], own_ref[place], other_ref[place])
                out_ref[64 * e : 64 * e + 32] = even
                out_ref[64 * e + 32 : 64 * (e + 1)] = odd
    else:
        out_ref = refs[0]
        attended_ref, attn_ref, stat_ref = refs[-3:]
    keys = kv_ref[pl.ds(step * TILE, TILE + WINDOW), :HD]
    values = kv_ref[pl.ds(step * TILE, TILE + WINDOW), HD:]
    values_t = values.T
    allowed = allowed_keys(spot_ref, start + step * TILE)
    for h in range(NH):
        columns = slice(HD * h, HD * (h + 1))
        scores = dot_bt(keys, query_ref[:, columns])
        expo = jnp.where(allowed, jnp.exp(scores), 0.0)
        total = jnp.sum(expo, axis=0, keepdims=True)
        mixed = dot(values_t, expo.astype(bf16)) * (1.0 / total)
        attended_ref[:, columns] = mixed.T.astype(bf16)
        stat_ref[h : h + 1, :] = jnp.log(total)
    attn_ref[...] = dot(attended_ref[...], out_ref[...])


def attend_call(start, spot, tab, query, kv, pieces, kept):
    tokens = query.shape[0]
    first = start // TILE
    unpacks = not kept
    outs = [
        jax.ShapeDtypeStruct((tokens, NH * HD), bf16),
        jax.ShapeDtypeStruct((tokens, D), f32),
        jax.ShapeDtypeStruct((8, tokens), f32),
    ]
    out_specs = [
        rows_of(NH * HD, first),
        rows_of(D, first),
        pl.BlockSpec((8, TILE), lambda i, *_: (0, i + first)),
    ]
    if unpacks:
        outs.append(jax.ShapeDtypeStruct((NH * HD, D), bf16))
        out_specs.append(whole((NH * HD, D)))
    return pl.pallas_call(
        functools.partial(attend_kernel, start, unpacks),
        grid_spec=pltpu.PrefetchScalarGridSpec(
            num_scalar_prefetch=2,
            grid=(2,),
            in_specs=[rows_of(NH * HD, first), whole(kv.shape)]
            + [whole(one.shape) for one in pieces]
            + [pl.BlockSpec(memory_space=pl.ANY)] * len(kept),
            out_specs=out_specs,
        ),
        out_shape=outs,
        input_output_aliases={4 + len(pieces) + i: i for i in range(len(kept))},
        compiler_params=params(48),
        cost_estimate=pl.CostEstimate(flops=7 * 10**9, bytes_accessed=8 << 20, transcendentals=1 << 21),
        name="attend",
    )(spot, tab, query, kv, *pieces, *kept)


def ffn_kernel(
    tab_ref, tab_back_ref, tab_down_ref, hidden_ref, attn_ref, cot_ref, gain_ref,
    packed_ref, down_ref,
    output_ref, dmid_ref, dattn_ref, dgain_ref, gate_keep_ref, gate_send_ref, up_keep_ref, up_send_ref,
    down_keep_ref, down_send_ref,
    middle_ref, normed_ref, normed_t_ref, sum_ref, dffn_ref, gate_w, up_w, down_w, inner_ref, slope_ref, act_ref,
):
    step = pl.program_id(0)
    tokens = hidden_ref.shape[0]
    parts = tokens // TILE
    chunks = FF // CHUNK
    core = tab_ref[PIECES // 2]

    @pl.when(step == 0)
    def _():
        def one(part, _):
            rows = pl.ds(pl.multiple_of(part * TILE, TILE), TILE)
            branch = attn_ref[rows]
            middle = hidden_ref[rows].astype(f32) + branch * inv_rms(branch) * gain_ref[1:2]
            middle_ref[rows] = middle
            normed_ref[rows] = (middle * inv_rms(middle) * gain_ref[2:3]).astype(bf16)
            return 0

        lax.fori_loop(0, parts, one, 0)
        normed_t_ref[...] = normed_ref[...].T

    @pl.when(step < chunks)
    def _():
        for d in range(PIECES):
            for j in range(CHUNK // LANES):
                columns = slice(LANES * j, LANES * (j + 1))
                rows = slice(ROWS * d, ROWS * (d + 1))
                gate_w[step, rows, columns] = packed_ref[d, ROWS * j : ROWS * (j + 1)]
                up_w[step, rows, columns] = packed_ref[d, 80 + ROWS * j : 80 + ROWS * (j + 1)]
        for i in range(CHUNK // 64):
            for g in range(D // LANES):
                down_w[step, 64 * i : 64 * (i + 1), LANES * g : LANES * (g + 1)] = down_ref[
                    i, 64 * g : 64 * (g + 1)
                ]
        for part in range(parts):
            rows = slice(part * TILE, (part + 1) * TILE)
            gate = dot(normed_ref[rows], gate_w[step])
            upward = dot(normed_ref[rows], up_w[step])
            square = gate * gate
            c0 = 0.7978845608028654
            c1 = c0 * 0.044715
            half = 0.5 * jnp.tanh(gate * (c0 + c1 * square)) + 0.5
            active = gate * half
            slope = half + 2.0 * active * (1.0 - half) * (c0 + 3.0 * c1 * square)
            inner = (active * upward).astype(bf16)
            inner_ref[step, rows] = inner
            act_ref[step, rows] = active.astype(bf16)
            slope_ref[step, rows] = (slope * upward).astype(bf16)
            more = dot(inner, down_w[step])

            @pl.when(step == 0)
            def _():
                sum_ref[rows] = more

            @pl.when(step > 0)
            def _():
                sum_ref[rows] += more

    @pl.when(step == chunks - 1)
    def _():
        def one(part, total):
            rows = pl.ds(pl.multiple_of(part * TILE, TILE), TILE)
            branch = sum_ref[rows]
            inverse = inv_rms(branch)
            grad = cot_ref[rows].astype(f32)
            output_ref[rows] = (middle_ref[rows] + branch * inverse * gain_ref[3:4]).astype(bf16)
            dffn_ref[rows] = rms_back(branch, inverse, gain_ref[3:4], grad).astype(bf16)
            return total + jnp.sum(grad * branch * inverse, axis=0, keepdims=True)

        dgain_ref[...] = jnp.zeros_like(dgain_ref)
        dgain_ref[3:4] = lax.fori_loop(0, parts, one, jnp.zeros((1, D), f32))

    @pl.when(step >= chunks)
    def _():
        chunk = step - chunks
        d_inner = dot_bt(dffn_ref[...], down_w[chunk])
        d_gate = (d_inner * slope_ref[chunk].astype(f32)).astype(bf16)
        d_up = (d_inner * act_ref[chunk].astype(f32)).astype(bf16)
        more = dot_bt(d_gate, gate_w[chunk]) + dot_bt(d_up, up_w[chunk])

        @pl.when(chunk == 0)
        def _():
            sum_ref[...] = more

        @pl.when(chunk > 0)
        def _():
            sum_ref[...] += more

        for grad_in, place_ref, keep_ref, send_ref in (
            (d_gate, tab_ref, gate_keep_ref, gate_send_ref), (d_up, tab_back_ref, up_keep_ref, up_send_ref),
        ):
            for j in range(CHUNK // LANES // 2):
                grad = dot(normed_t_ref[...], grad_in[:, 256 * j : 256 * (j + 1)])
                for k in range(2):
                    low = ROWS * (2 * j + k)
                    for e in range(PIECES // 2):
                        even = grad[2 * ROWS * e : 2 * ROWS * e + ROWS, LANES * k : LANES * (k + 1)]
                        odd = grad[2 * ROWS * e + ROWS : 2 * ROWS * (e + 1), LANES * k : LANES * (k + 1)]
                        even, odd = pair_of(core, even, odd)
                        keep_ref[place_ref[e], 0, low : low + ROWS] = even.astype(bf16)
                        send_ref[place_ref[e], 0, low : low + ROWS] = odd.astype(bf16)
        grad = dot_at(inner_ref[chunk], dffn_ref[...])
        for i in range(CHUNK // 128):
            place = tab_down_ref[chunk * (CHUNK // 128) + i]
            store_pair(
                down_keep_ref, down_send_ref, place, slice(0, 64), core,
                grad[128 * i : 128 * i + 64], grad[128 * i + 64 : 128 * (i + 1)],
            )

    @pl.when(step == 2 * chunks - 1)
    def _():
        def one(part, totals):
            rows = pl.ds(pl.multiple_of(part * TILE, TILE), TILE)
            middle = middle_ref[rows]
            inverse = inv_rms(middle)
            grad = sum_ref[rows]
            d_mid = cot_ref[rows].astype(f32) + rms_back(middle, inverse, gain_ref[2:3], grad)
            pre = jnp.sum(grad * middle * inverse, axis=0, keepdims=True)
            branch = attn_ref[rows]
            inverse = inv_rms(branch)
            dmid_ref[rows] = d_mid
            dattn_ref[rows] = rms_back(branch, inverse, gain_ref[1:2], d_mid).astype(bf16)
            mid = jnp.sum(d_mid * branch * inverse, axis=0, keepdims=True)
            return totals[0] + mid, totals[1] + pre

        zero = jnp.zeros((1, D), f32)
        mid, pre = lax.fori_loop(0, parts, one, (zero, zero))
        dgain_ref[1:2] = mid
        dgain_ref[2:3] = pre


def ffn_call(tabs, hidden, attn_out, cotangent, gains, packed):
    tokens = hidden.shape[0]
    chunks = FF // CHUNK
    pairs = PIECES // 2
    once = pl.Buffered(1)

    def single(shape):
        return pl.BlockSpec(shape, lambda i, *_: (0,) * len(shape), pipeline_mode=once)

    return pl.pallas_call(
        ffn_kernel,
        grid_spec=pltpu.PrefetchScalarGridSpec(
            num_scalar_prefetch=len(tabs),
            grid=(2 * chunks,),
            in_specs=[
                single((tokens, D)), single((tokens, D)), single((tokens, D)), whole((8, D)),
                pl.BlockSpec((PIECES, 160, LANES), lambda i, *_: (0, jnp.minimum(i, chunks - 1), 0)),
                pl.BlockSpec((8, 320, LANES), lambda i, *_: (jnp.minimum(i, chunks - 1), 2, 0)),
            ],
            out_specs=[
                single((tokens, D)), single((tokens, D)), single((tokens, D)), whole((8, D)),
                *[pl.BlockSpec((pairs, 1, 80, LANES), lambda i, *_: (0, jnp.maximum(i - chunks, 0), 0, 0))] * 4,
                single((pairs, 64, D)), single((pairs, 64, D)),
            ],
            scratch_shapes=[
                pltpu.VMEM((tokens, D), f32),
                pltpu.VMEM((tokens, D), bf16),
                pltpu.VMEM((D, tokens), bf16),
                pltpu.VMEM((tokens, D), f32),
                pltpu.VMEM((tokens, D), bf16),
                pltpu.VMEM((chunks, D, CHUNK), bf16),
                pltpu.VMEM((chunks, D, CHUNK), bf16),
                pltpu.VMEM((chunks, CHUNK, D), bf16),
                pltpu.VMEM((chunks, tokens, CHUNK), bf16),
                pltpu.VMEM((chunks, tokens, CHUNK), bf16),
                pltpu.VMEM((chunks, tokens, CHUNK), bf16),
            ],
        ),
        out_shape=[
            jax.ShapeDtypeStruct((tokens, D), bf16),
            jax.ShapeDtypeStruct((tokens, D), f32),
            jax.ShapeDtypeStruct((tokens, D), bf16),
            jax.ShapeDtypeStruct((8, D), f32),
            *[jax.ShapeDtypeStruct((pairs, chunks, 80, LANES), bf16)] * 4,
            jax.ShapeDtypeStruct((pairs, 64, D), bf16),
            jax.ShapeDtypeStruct((pairs, 64, D), bf16),
        ],
        compiler_params=params(60),
        cost_estimate=pl.CostEstimate(flops=60 * 10**9, bytes_accessed=30 << 20, transcendentals=tokens * FF),
        name="feed_forward",
    )(*tabs, hidden, attn_out, cotangent, gains, packed, packed)


def out_kernel(tab_ref, dattn_ref, attended_ref, keep_ref, send_ref):
    core = tab_ref[PIECES // 2]
    for b in range(NH * HD // 256):
        grad = dot_at(attended_ref[:, 256 * b : 256 * (b + 1)], dattn_ref[...])
        for i in range(4):
            store_pair(
                keep_ref, send_ref, tab_ref[4 * b + i], slice(0, 32), core,
                grad[64 * i : 64 * i + 32], grad[64 * i + 32 : 64 * (i + 1)],
            )


def out_call(tab, d_attn, attended):
    pairs = PIECES // 2
    return pl.pallas_call(
        out_kernel,
        grid_spec=pltpu.PrefetchScalarGridSpec(
            num_scalar_prefetch=1,
            grid=(1,),
            in_specs=[whole(d_attn.shape), whole(attended.shape)],
            out_specs=[whole((pairs, 32, D)), whole((pairs, 32, D))],
        ),
        out_shape=[
            jax.ShapeDtypeStruct((pairs, 32, D), bf16),
            jax.ShapeDtypeStruct((pairs, 32, D), bf16),
        ],
        compiler_params=params(48),
        cost_estimate=pl.CostEstimate(flops=4 * 10**9, bytes_accessed=8 << 20, transcendentals=0),
        name="out_gradient",
    )(tab, d_attn, attended)


def attend_back_kernel(
    start, spot_ref, query_ref, kv_ref, dattn_ref, out_ref, stat_ref, raw_ref, cos_ref, sin_ref, head_ref, *refs
):
    dquery_ref, dgain_ref, dkv_ref = refs[-3:]
    step = pl.program_id(0)

    @pl.when(step == 0)
    def _():
        dkv_ref[...] = jnp.zeros_like(dkv_ref)
        dgain_ref[...] = jnp.zeros_like(dgain_ref)

    span = pl.ds(step * TILE, TILE + WINDOW)
    keys = kv_ref[span, :HD]
    values = kv_ref[span, HD:]
    keys_t = keys.T
    allowed = allowed_keys(spot_ref, start + step * TILE)
    cosine = cos_ref[...]
    sine = sin_ref[...]
    gain = head_ref[0:1]
    d_gain = jnp.zeros((1, HD), f32)
    for h in range(NH):
        columns = slice(HD * h, HD * (h + 1))
        query = query_ref[:, columns]
        grad = dot_bt(dattn_ref[...], out_ref[columns]).astype(bf16)
        scores = dot_bt(keys, query) - stat_ref[h : h + 1, :]
        probs = jnp.where(allowed, jnp.exp(scores), 0.0)
        d_probs = dot_bt(values, grad)
        inside = jnp.sum(probs * d_probs, axis=0, keepdims=True)
        d_scores = (probs * (d_probs - inside)).astype(bf16)
        dkv_ref[span, HD:] += dot(probs.astype(bf16), grad)
        dkv_ref[span, :HD] += dot(d_scores, query)
        turned = dot(keys_t, d_scores).T * SCALE
        first, second = turned[:, :HALF], turned[:, HALF:]
        turned = jnp.concatenate(
            [first * cosine + second * sine, second * cosine - first * sine], axis=1
        )
        raw = raw_ref[:, columns]
        inverse = inv_rms(raw)
        dquery_ref[:, columns] = rms_back(raw, inverse, gain, turned).astype(bf16)
        d_gain = d_gain + jnp.sum(turned * raw * inverse, axis=0, keepdims=True)
    dgain_ref[0:1] += d_gain


def attend_back_call(start, spot, query, kv, d_attn, out, stat, query_raw, cosine, sine, heads, kept):
    tokens = query.shape[0]
    first = start // TILE
    return pl.pallas_call(
        functools.partial(attend_back_kernel, start),
        grid_spec=pltpu.PrefetchScalarGridSpec(
            num_scalar_prefetch=1,
            grid=(2,),
            in_specs=[
                rows_of(NH * HD, first), whole(kv.shape), rows_of(D, first), whole(out.shape),
                pl.BlockSpec((8, TILE), lambda i, *_: (0, i + first)),
                rows_of(NH * HD, first), rows_of(HALF, first), rows_of(HALF, first), whole((8, HD)),
            ]
            + [pl.BlockSpec(memory_space=pl.ANY)] * len(kept),
            out_specs=[rows_of(NH * HD, first), whole((8, HD)), whole(kv.shape)],
        ),
        out_shape=[
            jax.ShapeDtypeStruct((tokens, NH * HD), bf16),
            jax.ShapeDtypeStruct((8, HD), f32),
            jax.ShapeDtypeStruct(kv.shape, f32),
        ],
        input_output_aliases={10 + i: i for i in range(len(kept))},
        compiler_params=params(48),
        cost_estimate=pl.CostEstimate(flops=12 * 10**9, bytes_accessed=10 << 20, transcendentals=1 << 21),
        name="attend_backward",
    )(spot, query, kv, d_attn, out, stat, query_raw, cosine, sine, heads, *kept)


def qkv_grad_kernel(
    tab_ref, hidden_ref, gain_ref, head_ref, dquery_ref, near_ref, early_ref, halo_ref, key_raw_ref,
    cos_ref, sin_ref, weight_ref, dffn_gain_ref, dhead0_ref, dhead1_ref,
    dqkv_out_ref, keep_ref, send_ref, normed_ref, dqkv_ref, dkey_ref,
):
    step = pl.program_id(0)
    rows = pl.ds(pl.multiple_of(step * TILE, TILE), TILE)
    core = tab_ref[PIECES // 2]

    @pl.when(step == 0)
    def _():
        dkey_ref[...] = jnp.zeros_like(dkey_ref)

    inputs = hidden_ref[...].astype(f32)
    normed_ref[rows] = (inputs * inv_rms(inputs) * gain_ref[0:1]).astype(bf16)
    d_kv = near_ref[...] + jnp.where(step < 2, early_ref[...], halo_ref[...].astype(f32))
    cosine = cos_ref[...]
    sine = sin_ref[...]
    first, second = d_kv[:, :HALF], d_kv[:, HALF:HD]
    turned = jnp.concatenate(
        [first * cosine + second * sine, second * cosine - first * sine], axis=1
    )
    raw = key_raw_ref[...]
    raw_inverse = inv_rms(raw)
    dkey_ref[0:1] += jnp.sum(turned * raw * raw_inverse, axis=0, keepdims=True)
    d_key = rms_back(raw, raw_inverse, head_ref[1:2], turned).astype(bf16)
    all_three = jnp.concatenate([dquery_ref[...], d_key, d_kv[:, HD:].astype(bf16)], axis=1)
    dqkv_ref[rows] = all_three
    dqkv_out_ref[...] = all_three

    @pl.when(step == pl.num_programs(0) - 1)
    def _():
        weighted = jnp.zeros((D, LANES), f32)
        for h in range(4):
            rows_h = slice(ROWS * h, ROWS * (h + 1))
            grad = dot_at(normed_ref[...], dqkv_ref[:, GROUP * h : GROUP * (h + 1)])
            product = grad * weight_ref[:, GROUP * h : GROUP * (h + 1)].astype(f32)
            for j in range(GROUP // LANES):
                weighted = weighted + product[:, LANES * j : LANES * (j + 1)]
            for e in range(PIECES // 2):
                even = grad[2 * ROWS * e : 2 * ROWS * e + ROWS]
                odd = grad[2 * ROWS * e + ROWS : 2 * ROWS * (e + 1)]
                place = tab_ref[e]
                mine, theirs = pair_of(core, even, odd)
                keep_ref[place, rows_h] = mine.astype(bf16)
                send_ref[place, rows_h] = theirs.astype(bf16)
        d_gain_in = jnp.sum(weighted.T, axis=0, keepdims=True) / gain_ref[0:1]
        gains = jnp.concatenate(
            [
                d_gain_in, dffn_gain_ref[1:2], dffn_gain_ref[2:3], dffn_gain_ref[3:4],
                dhead0_ref[0:1] + dhead1_ref[0:1], dkey_ref[0:1],
            ],
            axis=1,
        )
        piece = gains.shape[1] // PIECES
        for e in range(PIECES // 2):
            even = jnp.broadcast_to(gains[:, 2 * piece * e : 2 * piece * e + piece], (8, piece))
            odd = jnp.broadcast_to(gains[:, 2 * piece * e + piece : 2 * piece * (e + 1)], (8, piece))
            place = tab_ref[e]
            keep_ref[place, 80:88] = jnp.zeros((8, GROUP), bf16)
            send_ref[place, 80:88] = jnp.zeros((8, GROUP), bf16)
            even, odd = pair_of(core, even, odd)
            keep_ref[place, 80:88, 0:piece] = even.astype(bf16)
            send_ref[place, 80:88, 0:piece] = odd.astype(bf16)


def qkv_grad_call(
    tab, hidden, gains, heads, d_query, near, early, halo, key_raw, cosine, sine, weight, d_gains, d_head0, d_head1
):
    tokens = hidden.shape[0]
    pairs = PIECES // 2
    last = WINDOW // TILE
    return pl.pallas_call(
        qkv_grad_kernel,
        grid_spec=pltpu.PrefetchScalarGridSpec(
            num_scalar_prefetch=1,
            grid=(tokens // TILE,),
            in_specs=[
                rows_of(D), whole((8, D)), whole((8, HD)), rows_of(NH * HD), rows_of(2 * HD),
                pl.BlockSpec((TILE, 2 * HD), lambda i, *_: (jnp.minimum(i + last, 2 * last - 1), 0)),
                pl.BlockSpec((TILE, 2 * HD), lambda i, *_: (jnp.clip(i - last, 0, last - 1), 0)),
                rows_of(HD), rows_of(HALF), rows_of(HALF), whole((D, QKV)),
                whole((8, D)), whole((8, HD)), whole((8, HD)),
            ],
            out_specs=[rows_of(QKV), whole((pairs, 88, GROUP)), whole((pairs, 88, GROUP))],
            scratch_shapes=[
                pltpu.VMEM((tokens, D), bf16),
                pltpu.VMEM((tokens, QKV), bf16),
                pltpu.VMEM((8, HD), f32),
            ],
        ),
        out_shape=[
            jax.ShapeDtypeStruct((tokens, QKV), bf16),
            jax.ShapeDtypeStruct((pairs, 88, GROUP), bf16),
            jax.ShapeDtypeStruct((pairs, 88, GROUP), bf16),
        ],
        compiler_params=params(48),
        cost_estimate=pl.CostEstimate(flops=9 * 10**9, bytes_accessed=12 << 20, transcendentals=0),
        name="qkv_gradients",
    )(
        tab, hidden, gains, heads, d_query, near, early, halo, key_raw, cosine, sine, weight, d_gains,
        d_head0, d_head1,
    )


def input_grad_kernel(hidden_ref, gain_ref, dqkv_ref, weight_ref, dmid_ref, grad_ref):
    inputs = hidden_ref[...].astype(f32)
    d_normed = dot_bt(dqkv_ref[...], weight_ref[...])
    back = rms_back(inputs, inv_rms(inputs), gain_ref[0:1], d_normed)
    grad_ref[...] = (dmid_ref[...] + back).astype(bf16)


def input_grad_call(hidden, gains, d_qkv, weight, d_mid):
    tokens = hidden.shape[0]
    return pl.pallas_call(
        input_grad_kernel,
        grid=(tokens // TILE,),
        in_specs=[rows_of(D), whole((8, D)), rows_of(QKV), whole((D, QKV)), rows_of(D)],
        out_specs=rows_of(D),
        out_shape=jax.ShapeDtypeStruct((tokens, D), bf16),
        compiler_params=params(48),
        cost_estimate=pl.CostEstimate(flops=6 * 10**9, bytes_accessed=10 << 20, transcendentals=0),
        name="input_gradient",
    )(hidden, gains, d_qkv, weight, d_mid)


def rotary_tables(positions):
    inverse = rope_base ** (-(jnp.arange(HALF, dtype=f32) * 2.0 / HD))
    angles = positions.astype(f32)[:, None] * inverse[None, :]
    return (jnp.cos(angles), jnp.sin(angles))


def per_device(
    hidden_in, segments, w_query, w_key, w_value, w_out, w_gate, w_up, w_down, norm_gains, cotangent
):
    tokens = hidden_in.shape[0]
    count = lax.axis_size("flat")
    near = count // PIECES
    me = lax.axis_index("flat") // near
    groups = [[p * near + i for i in range(near)] for p in range(PIECES)]
    shards = (w_query, w_key, w_value, w_out, w_gate, w_up, w_down, norm_gains)
    if near > 1:
        shards = [
            lax.all_gather(one, "flat", axis=0, tiled=True, axis_index_groups=groups) for one in shards
        ]
    s_query, s_key, s_value, s_out, s_gate, s_up, s_down, s_gain = shards

    gate_up = jnp.stack([s_gate.reshape(ROWS, -1, 4, LANES), s_up.reshape(ROWS, -1, 4, LANES)], axis=2)
    gate_up = gate_up.transpose(1, 2, 3, 0, 4).reshape(-1, LANES)
    down = s_down.reshape(-1, D // LANES, LANES).transpose(1, 0, 2).reshape(-1, LANES)
    columns = [[p * near + i for p in range(PIECES)] for i in range(near)]
    ffn_packed = lax.all_gather(
        jnp.concatenate([gate_up, down]), "flat", axis=0, tiled=False,
        axis_index_groups=columns if near > 1 else None,
    )

    qkv = jnp.concatenate(
        [s_query.reshape(ROWS, -1), s_key.reshape(ROWS, -1), s_value.reshape(ROWS, -1)], axis=1
    )
    gain_row = jnp.pad(s_gain[None], ((0, 7), (0, GROUP - s_gain.shape[0])))
    qkv = jnp.concatenate([qkv[:, GROUP * h : GROUP * (h + 1)] for h in range(4)] + [gain_row])
    over_z = (8, 16, 24)
    over_plane = (2, 4, 6)
    tab = chip_table(me, (8, 16, 2, 4))
    held = spread(qkv[None], over_z)
    held_out = spread(after(s_out.reshape(-1, D)[None], held), over_z)
    held = spread(held, over_plane)
    qkv_packed = (held, swapped(held, 1))
    held_out = spread(after(held_out, held), over_plane)
    pieces = jnp.stack([one[:, 80, : s_gain.shape[0]] for one in qkv_packed], axis=1)
    pieces = jnp.where((me & 1) == 0, pieces, pieces[:, ::-1])
    gain_all = jnp.take(pieces, tab[: PIECES // 2], axis=0).astype(f32).reshape(-1)
    gains = jnp.pad(gain_all[: 4 * D].reshape(4, D), ((0, 4), (0, 0)))
    heads = jnp.pad(gain_all[4 * D :].reshape(2, HD), ((0, 6), (0, 0)))

    rise = jnp.sum((segments == segments[0]).astype(jnp.int32))
    told = shifted(jnp.stack([segments[tokens - 1] + 1, tokens - rise]), 1)
    ahead = jnp.where(told[0] == segments[0] + 1, told[1], 0)
    index = jnp.arange(tokens, dtype=jnp.int32)
    positions = jnp.where(index < rise, index + ahead, index - rise)
    spot = jnp.stack([rise, ahead]).astype(jnp.int32)
    cosine, sine = rotary_tables(positions)

    query, kv, query_raw, key_raw, weight = qkv_call(
        tab, hidden_in, gains, heads, qkv_packed, cosine, sine
    )
    kv_prev = shifted(kv[tokens - WINDOW :], 1)
    held_out = after(held_out, query)
    *upper, out = attend_call(
        tokens - 2 * TILE, spot, tab, query, kv, (held_out, swapped(held_out, 1)), ()
    )
    kv_low = jnp.concatenate([after(kv_prev, *upper), kv[: tokens - WINDOW]])
    attended, attn_out, stat = attend_call(0, spot, tab, query, kv_low, (out,), upper)

    routes = ((2, 4, 8, 16), (4, 8, 2, 16), (8, 2, 4, 16))
    tabs = [chip_table(me, route[::-1]) for route in routes]
    output, d_mid, d_attn, d_gains, *pieces = ffn_call(
        tabs, hidden_in, attn_out, cotangent, gains, ffn_packed
    )
    came = [swapped(pieces[2 * i + 1], 1) for i in range(3)]
    keep_out, send_out = out_call(tabs[2], d_attn, attended)
    came.append(swapped(send_out, 1))
    d_query, d_head0, dkv_low = attend_back_call(
        0, spot, query, kv_low, after(d_attn, send_out), out, stat, query_raw, cosine, sine, heads, ()
    )
    came = [after(one, dkv_low) for one in came]
    held = [(pieces[0], came[0]), (pieces[2], came[1])]
    held.append((jnp.concatenate([pieces[4], keep_out], axis=1), jnp.concatenate(came[2:], axis=1)))
    halo = shifted(dkv_low[:WINDOW].astype(bf16), -1)
    halves = halved(held, routes, 0)
    d_query, d_head1, dkv_high = attend_back_call(
        tokens - 2 * TILE, spot, query, kv, after(d_attn, *[one[1] for one in halves]), out, stat,
        query_raw, cosine, sine, heads, (d_query,),
    )
    held = sent(halves, dkv_high)
    halves = halved(held, routes, 1)
    d_qkv, keep_qkv, send_qkv = qkv_grad_call(
        tab, after(hidden_in, *[one[1] for one in halves]), gains, heads, d_query, dkv_high, dkv_low, halo,
        key_raw, cosine, sine, weight, d_gains, d_head0, d_head1,
    )
    held = sent(halves, keep_qkv)
    halves = halved(held, routes, 2)
    grad_in = input_grad_call(
        after(hidden_in, *[one[1] for one in halves]), gains, after(d_qkv, send_qkv), weight, d_mid
    )
    total = keep_qkv.astype(f32) + after(swapped(send_qkv, 1), grad_in).astype(f32)
    held = sent(halves, grad_in)
    halves = halved(held, routes, 3)
    total = after(total, *[one[1] for one in halves])
    total = collected(total, over_plane)
    sum_gate, sum_up, sum_down = settled(sent(halves))
    sum_qkv = collected(total, over_z)[0]
    sum_down, sum_out = sum_down[:64], sum_down[64:]

    gate_up = [one.reshape(-1, ROWS, LANES).transpose(1, 0, 2).reshape(-1) for one in (sum_gate, sum_up)]
    parts = sum_qkv[: 4 * ROWS].reshape(4, ROWS, GROUP).transpose(1, 0, 2).reshape(ROWS, QKV)
    summed = (
        parts[:, : NH * HD].reshape(-1),
        parts[:, NH * HD : NH * HD + HD].reshape(-1),
        parts[:, NH * HD + HD :].reshape(-1),
        sum_out.reshape(-1),
        gate_up[0],
        gate_up[1],
        sum_down.reshape(-1),
        sum_qkv[4 * ROWS, : s_gain.shape[0]],
    )
    if near > 1:
        summed = tuple(
            lax.psum_scatter(one, "flat", scatter_dimension=0, tiled=True, axis_index_groups=groups)
            for one in summed
        )
    return (output, grad_in) + tuple(summed)


def solution(mesh):
    rows = P("flat", None)
    flat = P("flat")
    return jax.shard_map(
        per_device,
        mesh=mesh,
        in_specs=(rows,) + (flat,) * 9 + (rows,),
        out_specs=(rows, rows) + (flat,) * 8,
        check_vma=False,
    )
```

```python
import functools

import jax
import jax.numpy as jnp
from jax import lax
from jax.experimental import pallas as pl
from jax.experimental.pallas import tpu as pltpu
from jax.sharding import PartitionSpec as P

D = 640
NH = 4
HD = 256
FF = 2048
WINDOW = 512

PIECES = 32
ROWS = D // PIECES
TILE = 256
QKV = (NH + 2) * HD
GROUP = QKV // 4
CHUNK = 512
LANES = 128
HALF = HD // 2
SCALE = HD ** (-0.5)

epsilon = 1e-06
rope_base = 10000.0

bf16 = jnp.bfloat16
f32 = jnp.float32


def params(megabytes):
    return pltpu.CompilerParams(vmem_limit_bytes=megabytes << 20)


def whole(shape, space=None):
    return pl.BlockSpec(shape, lambda i, *_: (0,) * len(shape))


def rows_of(width, first=0):
    return pl.BlockSpec((TILE, width), lambda i, *_: (i + first, 0))


def shifted(block, distance):
    devices = range(lax.axis_size("flat"))
    route = [(i - distance, i) for i in devices if i - distance in devices]
    return lax.ppermute(block, "flat", route)


def swapped(block, mask):
    count = lax.axis_size("flat")
    near = count // PIECES
    route = [(i, ((i // near) ^ mask) * near + i % near) for i in range(count)]
    return lax.ppermute(block, "flat", route)


def after(value, *others):
    return lax.optimization_barrier((value,) + others)[0] if others else value


def spread(held, masks, *beside):
    return jnp.concatenate([held] + [after(swapped(held, mask), *beside) for mask in masks])


def collected(total, masks):
    size = total.shape[0] // (len(masks) + 1)
    came = [
        swapped(total[size * (i + 1) : size * (i + 2)].astype(bf16), mask) for i, mask in enumerate(masks)
    ]
    own = total[:size].astype(f32)
    for one in came:
        own = own + one.astype(f32)
    return own


def chip_table(me, order):
    differ = (me >> 1) ^ jnp.arange(PIECES // 2, dtype=jnp.int32)
    place = jnp.zeros((PIECES // 2,), jnp.int32)
    for step, mask in enumerate(order):
        place = place + jnp.where((differ & (mask >> 1)) != 0, 1 << step, 0)
    return jnp.concatenate([place, (me & 1)[None]]).astype(jnp.int32)


def halved(held, routes, step):
    half = 1 << (3 - step)
    nxt = []
    for (keep, other), route in zip(held, routes):
        away = (keep[half:].astype(f32) + other[half:].astype(f32)).astype(bf16)
        stay = (keep[:half].astype(f32) + other[:half].astype(f32)).astype(bf16)
        nxt.append((stay, away, route[step]))
    return nxt


def sent(halves, *beside):
    return [(stay, after(swapped(away, mask), *beside)) for stay, away, mask in halves]


def settled(held):
    return [(keep.astype(f32) + other.astype(f32))[0] for keep, other in held]


def dot(left, right):
    return lax.dot_general(left, right, (((1,), (0,)), ((), ())), preferred_element_type=f32)


def dot_bt(left, right):
    return lax.dot_general(left, right, (((1,), (1,)), ((), ())), preferred_element_type=f32)


def dot_at(left, right):
    return lax.dot_general(left, right, (((0,), (0,)), ((), ())), preferred_element_type=f32)


def inv_rms(values):
    return lax.rsqrt(jnp.mean(values * values, axis=-1, keepdims=True) + epsilon)


def rms_back(values, inverse, gain, grad):
    scaled = grad * gain
    mean = jnp.mean(scaled * values, axis=-1, keepdims=True)
    return inverse * scaled - values * (inverse * inverse * inverse * mean)


def store_pair(keep, send, index, rows, core, even, odd):
    mine, theirs = pair_of(core, even, odd)
    keep[index, rows] = mine.astype(bf16)
    send[index, rows] = theirs.astype(bf16)


def pair_of(core, own, other):
    mine = core == 0
    return jnp.where(mine, own, other), jnp.where(mine, other, own)


def qkv_kernel(
    tab_ref, hidden_ref, gain_ref, head_ref, own_ref, other_ref, cos_ref, sin_ref,
    query_ref, kv_ref, query_raw_ref, key_raw_ref, weight_ref,
):
    @pl.when(pl.program_id(0) == 0)
    def _():
        core = tab_ref[PIECES // 2]
        for e in range(PIECES // 2):
            for d, block in zip((2 * e, 2 * e + 1), pair_of(core, own_ref[tab_ref[e]], other_ref[tab_ref[e]])):
                for h in range(4):
                    weight_ref[ROWS * d : ROWS * (d + 1), GROUP * h : GROUP * (h + 1)] = block[
                        ROWS * h : ROWS * (h + 1)
                    ]

    inputs = hidden_ref[...].astype(f32)
    normed = (inputs * inv_rms(inputs) * gain_ref[0:1]).astype(bf16)
    raw = dot(normed, weight_ref[...])
    cosine = cos_ref[...]
    sine = sin_ref[...]

    def turned(values, gain):
        values = values * inv_rms(values) * gain
        first, second = values[:, :HALF], values[:, HALF:]
        return jnp.concatenate(
            [first * cosine - second * sine, second * cosine + first * sine], axis=1
        )

    for h in range(NH):
        columns = slice(HD * h, HD * (h + 1))
        query_ref[:, columns] = (turned(raw[:, columns], head_ref[0:1]) * SCALE).astype(bf16)
    query_raw_ref[...] = raw[:, : NH * HD]
    key_raw = raw[:, NH * HD : NH * HD + HD]
    key_raw_ref[...] = key_raw
    kv_ref[:, :HD] = turned(key_raw, head_ref[1:2]).astype(bf16)
    kv_ref[:, HD:] = raw[:, NH * HD + HD :].astype(bf16)


def qkv_call(tab, hidden, gains, heads, pieces, cosine, sine):
    tokens = hidden.shape[0]
    return pl.pallas_call(
        qkv_kernel,
        grid_spec=pltpu.PrefetchScalarGridSpec(
            num_scalar_prefetch=1,
            grid=(tokens // TILE,),
            in_specs=[
                rows_of(D), whole((8, D)), whole((8, HD)), *[whole(one.shape) for one in pieces],
                rows_of(HALF), rows_of(HALF),
            ],
            out_specs=[
                rows_of(NH * HD), rows_of(2 * HD), rows_of(NH * HD), rows_of(HD),
                whole((D, QKV)),
            ],
        ),
        out_shape=[
            jax.ShapeDtypeStruct((tokens, NH * HD), bf16),
            jax.ShapeDtypeStruct((tokens, 2 * HD), bf16),
            jax.ShapeDtypeStruct((tokens, NH * HD), f32),
            jax.ShapeDtypeStruct((tokens, HD), f32),
            jax.ShapeDtypeStruct((D, QKV), bf16),
        ],
        compiler_params=params(48),
        cost_estimate=pl.CostEstimate(flops=9 * 10**9, bytes_accessed=20 << 20, transcendentals=0),
        name="qkv",
    )(tab, hidden, gains, heads, *pieces, cosine, sine)


def allowed_keys(spot_ref, first):
    token = lax.broadcasted_iota(jnp.int32, (1, TILE), 1)
    spot = token + first
    position = jnp.where(spot < spot_ref[0], spot + spot_ref[1], spot - spot_ref[0])
    lowest = token + WINDOW - jnp.minimum(position, WINDOW - 1)
    key = lax.broadcasted_iota(jnp.int32, (TILE + WINDOW, TILE), 0)
    return (key >= lowest) & (key <= token + WINDOW)


def attend_kernel(start, unpacks, spot_ref, tab_ref, query_ref, kv_ref, *refs):
    step = pl.program_id(0)
    if unpacks:
        own_ref, other_ref, attended_ref, attn_ref, stat_ref, out_ref = refs

        @pl.when(step == 0)
        def _():
            for e in range(PIECES // 2):
                place = tab_ref[e]
                even, odd = pair_of(tab_ref[PIECES // 2], own_ref[place], other_ref[place])
                out_ref[64 * e : 64 * e + 32] = even
                out_ref[64 * e + 32 : 64 * (e + 1)] = odd
    else:
        out_ref = refs[0]
        attended_ref, attn_ref, stat_ref = refs[-3:]
    keys = kv_ref[pl.ds(step * TILE, TILE + WINDOW), :HD]
    values = kv_ref[pl.ds(step * TILE, TILE + WINDOW), HD:]
    values_t = values.T
    allowed = allowed_keys(spot_ref, start + step * TILE)
    for h in range(NH):
        columns = slice(HD * h, HD * (h + 1))
        scores = dot_bt(keys, query_ref[:, columns])
        expo = jnp.where(allowed, jnp.exp(scores), 0.0)
        total = jnp.sum(expo, axis=0, keepdims=True)
        mixed = dot(values_t, expo.astype(bf16)) * (1.0 / total)
        attended_ref[:, columns] = mixed.T.astype(bf16)
        stat_ref[h : h + 1, :] = jnp.log(total)
    attn_ref[...] = dot(attended_ref[...], out_ref[...])


def attend_call(start, spot, tab, query, kv, pieces, kept):
    tokens = query.shape[0]
    first = start // TILE
    unpacks = not kept
    outs = [
        jax.ShapeDtypeStruct((tokens, NH * HD), bf16),
        jax.ShapeDtypeStruct((tokens, D), f32),
        jax.ShapeDtypeStruct((8, tokens), f32),
    ]
    out_specs = [
        rows_of(NH * HD, first),
        rows_of(D, first),
        pl.BlockSpec((8, TILE), lambda i, *_: (0, i + first)),
    ]
    if unpacks:
        outs.append(jax.ShapeDtypeStruct((NH * HD, D), bf16))
        out_specs.append(whole((NH * HD, D)))
    return pl.pallas_call(
        functools.partial(attend_kernel, start, unpacks),
        grid_spec=pltpu.PrefetchScalarGridSpec(
            num_scalar_prefetch=2,
            grid=(2,),
            in_specs=[rows_of(NH * HD, first), whole(kv.shape)]
            + [whole(one.shape) for one in pieces]
            + [pl.BlockSpec(memory_space=pl.ANY)] * len(kept),
            out_specs=out_specs,
        ),
        out_shape=outs,
        input_output_aliases={4 + len(pieces) + i: i for i in range(len(kept))},
        compiler_params=params(48),
        cost_estimate=pl.CostEstimate(flops=7 * 10**9, bytes_accessed=8 << 20, transcendentals=1 << 21),
        name="attend",
    )(spot, tab, query, kv, *pieces, *kept)


def ffn_kernel(
    tab_ref, tab_back_ref, tab_down_ref, hidden_ref, attn_ref, cot_ref, gain_ref,
    packed_ref, down_ref,
    output_ref, dmid_ref, dattn_ref, dgain_ref, gate_keep_ref, gate_send_ref, up_keep_ref, up_send_ref,
    down_keep_ref, down_send_ref,
    middle_ref, normed_ref, normed_t_ref, sum_ref, dffn_ref, gate_w, up_w, down_w, inner_ref, slope_ref, act_ref,
):
    step = pl.program_id(0)
    tokens = hidden_ref.shape[0]
    parts = tokens // TILE
    chunks = FF // CHUNK
    core = tab_ref[PIECES // 2]

    @pl.when(step == 0)
    def _():
        def one(part, _):
            rows = pl.ds(pl.multiple_of(part * TILE, TILE), TILE)
            branch = attn_ref[rows]
            middle = hidden_ref[rows].astype(f32) + branch * inv_rms(branch) * gain_ref[1:2]
            middle_ref[rows] = middle
            normed_ref[rows] = (middle * inv_rms(middle) * gain_ref[2:3]).astype(bf16)
            return 0

        lax.fori_loop(0, parts, one, 0)
        normed_t_ref[...] = normed_ref[...].T

    @pl.when(step < chunks)
    def _():
        for d in range(PIECES):
            for j in range(CHUNK // LANES):
                columns = slice(LANES * j, LANES * (j + 1))
                rows = slice(ROWS * d, ROWS * (d + 1))
                gate_w[step, rows, columns] = packed_ref[d, ROWS * j : ROWS * (j + 1)]
                up_w[step, rows, columns] = packed_ref[d, 80 + ROWS * j : 80 + ROWS * (j + 1)]
        for i in range(CHUNK // 64):
            for g in range(D // LANES):
                down_w[step, 64 * i : 64 * (i + 1), LANES * g : LANES * (g + 1)] = down_ref[
                    i, 64 * g : 64 * (g + 1)
                ]
        for part in range(parts):
            rows = slice(part * TILE, (part + 1) * TILE)
            gate = dot(normed_ref[rows], gate_w[step])
            upward = dot(normed_ref[rows], up_w[step])
            square = gate * gate
            c0 = 0.7978845608028654
            c1 = c0 * 0.044715
            half = 0.5 * jnp.tanh(gate * (c0 + c1 * square)) + 0.5
            active = gate * half
            slope = half + 2.0 * active * (1.0 - half) * (c0 + 3.0 * c1 * square)
            inner = (active * upward).astype(bf16)
            inner_ref[step, rows] = inner
            act_ref[step, rows] = active.astype(bf16)
            slope_ref[step, rows] = (slope * upward).astype(bf16)
            more = dot(inner, down_w[step])

            @pl.when(step == 0)
            def _():
                sum_ref[rows] = more

            @pl.when(step > 0)
            def _():
                sum_ref[rows] += more

    @pl.when(step == chunks - 1)
    def _():
        def one(part, total):
            rows = pl.ds(pl.multiple_of(part * TILE, TILE), TILE)
            branch = sum_ref[rows]
            inverse = inv_rms(branch)
            grad = cot_ref[rows].astype(f32)
            output_ref[rows] = (middle_ref[rows] + branch * inverse * gain_ref[3:4]).astype(bf16)
            dffn_ref[rows] = rms_back(branch, inverse, gain_ref[3:4], grad).astype(bf16)
            return total + jnp.sum(grad * branch * inverse, axis=0, keepdims=True)

        dgain_ref[...] = jnp.zeros_like(dgain_ref)
        dgain_ref[3:4] = lax.fori_loop(0, parts, one, jnp.zeros((1, D), f32))

    @pl.when(step >= chunks)
    def _():
        chunk = step - chunks
        d_inner = dot_bt(dffn_ref[...], down_w[chunk])
        d_gate = (d_inner * slope_ref[chunk].astype(f32)).astype(bf16)
        d_up = (d_inner * act_ref[chunk].astype(f32)).astype(bf16)
        more = dot_bt(d_gate, gate_w[chunk]) + dot_bt(d_up, up_w[chunk])

        @pl.when(chunk == 0)
        def _():
            sum_ref[...] = more

        @pl.when(chunk > 0)
        def _():
            sum_ref[...] += more

        for grad_in, place_ref, keep_ref, send_ref in (
            (d_gate, tab_ref, gate_keep_ref, gate_send_ref), (d_up, tab_back_ref, up_keep_ref, up_send_ref),
        ):
            for j in range(CHUNK // LANES // 2):
                grad = dot(normed_t_ref[...], grad_in[:, 256 * j : 256 * (j + 1)])
                for k in range(2):
                    low = ROWS * (2 * j + k)
                    for e in range(PIECES // 2):
                        even = grad[2 * ROWS * e : 2 * ROWS * e + ROWS, LANES * k : LANES * (k + 1)]
                        odd = grad[2 * ROWS * e + ROWS : 2 * ROWS * (e + 1), LANES * k : LANES * (k + 1)]
                        even, odd = pair_of(core, even, odd)
                        keep_ref[place_ref[e], 0, low : low + ROWS] = even.astype(bf16)
                        send_ref[place_ref[e], 0, low : low + ROWS] = odd.astype(bf16)
        grad = dot_at(inner_ref[chunk], dffn_ref[...])
        for i in range(CHUNK // 128):
            place = tab_down_ref[chunk * (CHUNK // 128) + i]
            store_pair(
                down_keep_ref, down_send_ref, place, slice(0, 64), core,
                grad[128 * i : 128 * i + 64], grad[128 * i + 64 : 128 * (i + 1)],
            )

    @pl.when(step == 2 * chunks - 1)
    def _():
        def one(part, totals):
            rows = pl.ds(pl.multiple_of(part * TILE, TILE), TILE)
            middle = middle_ref[rows]
            inverse = inv_rms(middle)
            grad = sum_ref[rows]
            d_mid = cot_ref[rows].astype(f32) + rms_back(middle, inverse, gain_ref[2:3], grad)
            pre = jnp.sum(grad * middle * inverse, axis=0, keepdims=True)
            branch = attn_ref[rows]
            inverse = inv_rms(branch)
            dmid_ref[rows] = d_mid
            dattn_ref[rows] = rms_back(branch, inverse, gain_ref[1:2], d_mid).astype(bf16)
            mid = jnp.sum(d_mid * branch * inverse, axis=0, keepdims=True)
            return totals[0] + mid, totals[1] + pre

        zero = jnp.zeros((1, D), f32)
        mid, pre = lax.fori_loop(0, parts, one, (zero, zero))
        dgain_ref[1:2] = mid
        dgain_ref[2:3] = pre


def ffn_call(tabs, hidden, attn_out, cotangent, gains, packed):
    tokens = hidden.shape[0]
    chunks = FF // CHUNK
    pairs = PIECES // 2
    once = pl.Buffered(1)

    def single(shape):
        return pl.BlockSpec(shape, lambda i, *_: (0,) * len(shape), pipeline_mode=once)

    return pl.pallas_call(
        ffn_kernel,
        grid_spec=pltpu.PrefetchScalarGridSpec(
            num_scalar_prefetch=len(tabs),
            grid=(2 * chunks,),
            in_specs=[
                single((tokens, D)), single((tokens, D)), single((tokens, D)), whole((8, D)),
                pl.BlockSpec((PIECES, 160, LANES), lambda i, *_: (0, jnp.minimum(i, chunks - 1), 0)),
                pl.BlockSpec((8, 320, LANES), lambda i, *_: (jnp.minimum(i, chunks - 1), 2, 0)),
            ],
            out_specs=[
                single((tokens, D)), single((tokens, D)), single((tokens, D)), whole((8, D)),
                *[pl.BlockSpec((pairs, 1, 80, LANES), lambda i, *_: (0, jnp.maximum(i - chunks, 0), 0, 0))] * 4,
                single((pairs, 64, D)), single((pairs, 64, D)),
            ],
            scratch_shapes=[
                pltpu.VMEM((tokens, D), f32),
                pltpu.VMEM((tokens, D), bf16),
                pltpu.VMEM((D, tokens), bf16),
                pltpu.VMEM((tokens, D), f32),
                pltpu.VMEM((tokens, D), bf16),
                pltpu.VMEM((chunks, D, CHUNK), bf16),
                pltpu.VMEM((chunks, D, CHUNK), bf16),
                pltpu.VMEM((chunks, CHUNK, D), bf16),
                pltpu.VMEM((chunks, tokens, CHUNK), bf16),
                pltpu.VMEM((chunks, tokens, CHUNK), bf16),
                pltpu.VMEM((chunks, tokens, CHUNK), bf16),
            ],
        ),
        out_shape=[
            jax.ShapeDtypeStruct((tokens, D), bf16),
            jax.ShapeDtypeStruct((tokens, D), f32),
            jax.ShapeDtypeStruct((tokens, D), bf16),
            jax.ShapeDtypeStruct((8, D), f32),
            *[jax.ShapeDtypeStruct((pairs, chunks, 80, LANES), bf16)] * 4,
            jax.ShapeDtypeStruct((pairs, 64, D), bf16),
            jax.ShapeDtypeStruct((pairs, 64, D), bf16),
        ],
        compiler_params=params(60),
        cost_estimate=pl.CostEstimate(flops=60 * 10**9, bytes_accessed=30 << 20, transcendentals=tokens * FF),
        name="feed_forward",
    )(*tabs, hidden, attn_out, cotangent, gains, packed, packed)


def out_kernel(tab_ref, dattn_ref, attended_ref, keep_ref, send_ref):
    core = tab_ref[PIECES // 2]
    for b in range(NH * HD // 256):
        grad = dot_at(attended_ref[:, 256 * b : 256 * (b + 1)], dattn_ref[...])
        for i in range(4):
            store_pair(
                keep_ref, send_ref, tab_ref[4 * b + i], slice(0, 32), core,
                grad[64 * i : 64 * i + 32], grad[64 * i + 32 : 64 * (i + 1)],
            )


def out_call(tab, d_attn, attended):
    pairs = PIECES // 2
    return pl.pallas_call(
        out_kernel,
        grid_spec=pltpu.PrefetchScalarGridSpec(
            num_scalar_prefetch=1,
            grid=(1,),
            in_specs=[whole(d_attn.shape), whole(attended.shape)],
            out_specs=[whole((pairs, 32, D)), whole((pairs, 32, D))],
        ),
        out_shape=[
            jax.ShapeDtypeStruct((pairs, 32, D), bf16),
            jax.ShapeDtypeStruct((pairs, 32, D), bf16),
        ],
        compiler_params=params(48),
        cost_estimate=pl.CostEstimate(flops=4 * 10**9, bytes_accessed=8 << 20, transcendentals=0),
        name="out_gradient",
    )(tab, d_attn, attended)


def attend_back_kernel(
    start, spot_ref, query_ref, kv_ref, dattn_ref, out_ref, stat_ref, raw_ref, cos_ref, sin_ref, head_ref, *refs
):
    dquery_ref, dgain_ref, dkv_ref = refs[-3:]
    step = pl.program_id(0)

    @pl.when(step == 0)
    def _():
        dkv_ref[...] = jnp.zeros_like(dkv_ref)
        dgain_ref[...] = jnp.zeros_like(dgain_ref)

    span = pl.ds(step * TILE, TILE + WINDOW)
    keys = kv_ref[span, :HD]
    values = kv_ref[span, HD:]
    keys_t = keys.T
    allowed = allowed_keys(spot_ref, start + step * TILE)
    cosine = cos_ref[...]
    sine = sin_ref[...]
    gain = head_ref[0:1]
    d_gain = jnp.zeros((1, HD), f32)
    for h in range(NH):
        columns = slice(HD * h, HD * (h + 1))
        query = query_ref[:, columns]
        grad = dot_bt(dattn_ref[...], out_ref[columns]).astype(bf16)
        scores = dot_bt(keys, query) - stat_ref[h : h + 1, :]
        probs = jnp.where(allowed, jnp.exp(scores), 0.0)
        d_probs = dot_bt(values, grad)
        inside = jnp.sum(probs * d_probs, axis=0, keepdims=True)
        d_scores = (probs * (d_probs - inside)).astype(bf16)
        dkv_ref[span, HD:] += dot(probs.astype(bf16), grad)
        dkv_ref[span, :HD] += dot(d_scores, query)
        turned = dot(keys_t, d_scores).T * SCALE
        first, second = turned[:, :HALF], turned[:, HALF:]
        turned = jnp.concatenate(
            [first * cosine + second * sine, second * cosine - first * sine], axis=1
        )
        raw = raw_ref[:, columns]
        inverse = inv_rms(raw)
        dquery_ref[:, columns] = rms_back(raw, inverse, gain, turned).astype(bf16)
        d_gain = d_gain + jnp.sum(turned * raw * inverse, axis=0, keepdims=True)
    dgain_ref[0:1] += d_gain


def attend_back_call(start, spot, query, kv, d_attn, out, stat, query_raw, cosine, sine, heads, kept):
    tokens = query.shape[0]
    first = start // TILE
    return pl.pallas_call(
        functools.partial(attend_back_kernel, start),
        grid_spec=pltpu.PrefetchScalarGridSpec(
            num_scalar_prefetch=1,
            grid=(2,),
            in_specs=[
                rows_of(NH * HD, first), whole(kv.shape), rows_of(D, first), whole(out.shape),
                pl.BlockSpec((8, TILE), lambda i, *_: (0, i + first)),
                rows_of(NH * HD, first), rows_of(HALF, first), rows_of(HALF, first), whole((8, HD)),
            ]
            + [pl.BlockSpec(memory_space=pl.ANY)] * len(kept),
            out_specs=[rows_of(NH * HD, first), whole((8, HD)), whole(kv.shape)],
        ),
        out_shape=[
            jax.ShapeDtypeStruct((tokens, NH * HD), bf16),
            jax.ShapeDtypeStruct((8, HD), f32),
            jax.ShapeDtypeStruct(kv.shape, f32),
        ],
        input_output_aliases={10 + i: i for i in range(len(kept))},
        compiler_params=params(48),
        cost_estimate=pl.CostEstimate(flops=12 * 10**9, bytes_accessed=10 << 20, transcendentals=1 << 21),
        name="attend_backward",
    )(spot, query, kv, d_attn, out, stat, query_raw, cosine, sine, heads, *kept)


def qkv_grad_kernel(
    tab_ref, hidden_ref, gain_ref, head_ref, dquery_ref, near_ref, early_ref, halo_ref, key_raw_ref,
    cos_ref, sin_ref, weight_ref, dffn_gain_ref, dhead0_ref, dhead1_ref,
    dqkv_out_ref, keep_ref, send_ref, normed_ref, dqkv_ref, dkey_ref,
):
    step = pl.program_id(0)
    rows = pl.ds(pl.multiple_of(step * TILE, TILE), TILE)
    core = tab_ref[PIECES // 2]

    @pl.when(step == 0)
    def _():
        dkey_ref[...] = jnp.zeros_like(dkey_ref)

    inputs = hidden_ref[...].astype(f32)
    normed_ref[rows] = (inputs * inv_rms(inputs) * gain_ref[0:1]).astype(bf16)
    d_kv = near_ref[...] + jnp.where(step < 2, early_ref[...], halo_ref[...].astype(f32))
    cosine = cos_ref[...]
    sine = sin_ref[...]
    first, second = d_kv[:, :HALF], d_kv[:, HALF:HD]
    turned = jnp.concatenate(
        [first * cosine + second * sine, second * cosine - first * sine], axis=1
    )
    raw = key_raw_ref[...]
    raw_inverse = inv_rms(raw)
    dkey_ref[0:1] += jnp.sum(turned * raw * raw_inverse, axis=0, keepdims=True)
    d_key = rms_back(raw, raw_inverse, head_ref[1:2], turned).astype(bf16)
    all_three = jnp.concatenate([dquery_ref[...], d_key, d_kv[:, HD:].astype(bf16)], axis=1)
    dqkv_ref[rows] = all_three
    dqkv_out_ref[...] = all_three

    @pl.when(step == pl.num_programs(0) - 1)
    def _():
        weighted = jnp.zeros((D, LANES), f32)
        for h in range(4):
            rows_h = slice(ROWS * h, ROWS * (h + 1))
            grad = dot_at(normed_ref[...], dqkv_ref[:, GROUP * h : GROUP * (h + 1)])
            product = grad * weight_ref[:, GROUP * h : GROUP * (h + 1)].astype(f32)
            for j in range(GROUP // LANES):
                weighted = weighted + product[:, LANES * j : LANES * (j + 1)]
            for e in range(PIECES // 2):
                even = grad[2 * ROWS * e : 2 * ROWS * e + ROWS]
                odd = grad[2 * ROWS * e + ROWS : 2 * ROWS * (e + 1)]
                place = tab_ref[e]
                mine, theirs = pair_of(core, even, odd)
                keep_ref[place, rows_h] = mine.astype(bf16)
                send_ref[place, rows_h] = theirs.astype(bf16)
        d_gain_in = jnp.sum(weighted.T, axis=0, keepdims=True) / gain_ref[0:1]
        gains = jnp.concatenate(
            [
                d_gain_in, dffn_gain_ref[1:2], dffn_gain_ref[2:3], dffn_gain_ref[3:4],
                dhead0_ref[0:1] + dhead1_ref[0:1], dkey_ref[0:1],
            ],
            axis=1,
        )
        piece = gains.shape[1] // PIECES
        for e in range(PIECES // 2):
            even = jnp.broadcast_to(gains[:, 2 * piece * e : 2 * piece * e + piece], (8, piece))
            odd = jnp.broadcast_to(gains[:, 2 * piece * e + piece : 2 * piece * (e + 1)], (8, piece))
            place = tab_ref[e]
            keep_ref[place, 80:88] = jnp.zeros((8, GROUP), bf16)
            send_ref[place, 80:88] = jnp.zeros((8, GROUP), bf16)
            even, odd = pair_of(core, even, odd)
            keep_ref[place, 80:88, 0:piece] = even.astype(bf16)
            send_ref[place, 80:88, 0:piece] = odd.astype(bf16)


def qkv_grad_call(
    tab, hidden, gains, heads, d_query, near, early, halo, key_raw, cosine, sine, weight, d_gains, d_head0, d_head1
):
    tokens = hidden.shape[0]
    pairs = PIECES // 2
    last = WINDOW // TILE
    return pl.pallas_call(
        qkv_grad_kernel,
        grid_spec=pltpu.PrefetchScalarGridSpec(
            num_scalar_prefetch=1,
            grid=(tokens // TILE,),
            in_specs=[
                rows_of(D), whole((8, D)), whole((8, HD)), rows_of(NH * HD), rows_of(2 * HD),
                pl.BlockSpec((TILE, 2 * HD), lambda i, *_: (jnp.minimum(i + last, 2 * last - 1), 0)),
                pl.BlockSpec((TILE, 2 * HD), lambda i, *_: (jnp.clip(i - last, 0, last - 1), 0)),
                rows_of(HD), rows_of(HALF), rows_of(HALF), whole((D, QKV)),
                whole((8, D)), whole((8, HD)), whole((8, HD)),
            ],
            out_specs=[rows_of(QKV), whole((pairs, 88, GROUP)), whole((pairs, 88, GROUP))],
            scratch_shapes=[
                pltpu.VMEM((tokens, D), bf16),
                pltpu.VMEM((tokens, QKV), bf16),
                pltpu.VMEM((8, HD), f32),
            ],
        ),
        out_shape=[
            jax.ShapeDtypeStruct((tokens, QKV), bf16),
            jax.ShapeDtypeStruct((pairs, 88, GROUP), bf16),
            jax.ShapeDtypeStruct((pairs, 88, GROUP), bf16),
        ],
        compiler_params=params(48),
        cost_estimate=pl.CostEstimate(flops=9 * 10**9, bytes_accessed=12 << 20, transcendentals=0),
        name="qkv_gradients",
    )(
        tab, hidden, gains, heads, d_query, near, early, halo, key_raw, cosine, sine, weight, d_gains,
        d_head0, d_head1,
    )


def input_grad_kernel(hidden_ref, gain_ref, dqkv_ref, weight_ref, dmid_ref, grad_ref):
    inputs = hidden_ref[...].astype(f32)
    d_normed = dot_bt(dqkv_ref[...], weight_ref[...])
    back = rms_back(inputs, inv_rms(inputs), gain_ref[0:1], d_normed)
    grad_ref[...] = (dmid_ref[...] + back).astype(bf16)


def input_grad_call(hidden, gains, d_qkv, weight, d_mid):
    tokens = hidden.shape[0]
    return pl.pallas_call(
        input_grad_kernel,
        grid=(tokens // TILE,),
        in_specs=[rows_of(D), whole((8, D)), rows_of(QKV), whole((D, QKV)), rows_of(D)],
        out_specs=rows_of(D),
        out_shape=jax.ShapeDtypeStruct((tokens, D), bf16),
        compiler_params=params(48),
        cost_estimate=pl.CostEstimate(flops=6 * 10**9, bytes_accessed=10 << 20, transcendentals=0),
        name="input_gradient",
    )(hidden, gains, d_qkv, weight, d_mid)


def rotary_tables(positions):
    inverse = rope_base ** (-(jnp.arange(HALF, dtype=f32) * 2.0 / HD))
    angles = positions.astype(f32)[:, None] * inverse[None, :]
    return (jnp.cos(angles), jnp.sin(angles))


def per_device(
    hidden_in, segments, w_query, w_key, w_value, w_out, w_gate, w_up, w_down, norm_gains, cotangent
):
    tokens = hidden_in.shape[0]
    count = lax.axis_size("flat")
    near = count // PIECES
    me = lax.axis_index("flat") // near
    groups = [[p * near + i for i in range(near)] for p in range(PIECES)]
    shards = (w_query, w_key, w_value, w_out, w_gate, w_up, w_down, norm_gains)
    if near > 1:
        shards = [
            lax.all_gather(one, "flat", axis=0, tiled=True, axis_index_groups=groups) for one in shards
        ]
    s_query, s_key, s_value, s_out, s_gate, s_up, s_down, s_gain = shards

    gate_up = jnp.stack([s_gate.reshape(ROWS, -1, 4, LANES), s_up.reshape(ROWS, -1, 4, LANES)], axis=2)
    gate_up = gate_up.transpose(1, 2, 3, 0, 4).reshape(-1, LANES)
    down = s_down.reshape(-1, D // LANES, LANES).transpose(1, 0, 2).reshape(-1, LANES)
    columns = [[p * near + i for p in range(PIECES)] for i in range(near)]
    ffn_packed = lax.all_gather(
        jnp.concatenate([gate_up, down]), "flat", axis=0, tiled=False,
        axis_index_groups=columns if near > 1 else None,
    )

    qkv = jnp.concatenate(
        [s_query.reshape(ROWS, -1), s_key.reshape(ROWS, -1), s_value.reshape(ROWS, -1)], axis=1
    )
    gain_row = jnp.pad(s_gain[None], ((0, 7), (0, GROUP - s_gain.shape[0])))
    qkv = jnp.concatenate([qkv[:, GROUP * h : GROUP * (h + 1)] for h in range(4)] + [gain_row])
    over_z = (8, 16, 24)
    over_plane = (2, 4, 6)
    tab = chip_table(me, (8, 16, 2, 4))
    held = spread(qkv[None], over_z)
    held_out = spread(after(s_out.reshape(-1, D)[None], held), over_z)
    held = spread(held, over_plane)
    qkv_packed = (held, swapped(held, 1))
    pieces = jnp.stack([one[:, 80, : s_gain.shape[0]] for one in qkv_packed], axis=1)
    pieces = jnp.where((me & 1) == 0, pieces, pieces[:, ::-1])
    gain_all = jnp.take(pieces, tab[: PIECES // 2], axis=0).astype(f32).reshape(-1)
    gains = jnp.pad(gain_all[: 4 * D].reshape(4, D), ((0, 4), (0, 0)))
    heads = jnp.pad(gain_all[4 * D :].reshape(2, HD), ((0, 6), (0, 0)))

    rise = jnp.sum((segments == segments[0]).astype(jnp.int32))
    told = shifted(jnp.stack([segments[tokens - 1] + 1, tokens - rise]), 1)
    ahead = jnp.where(told[0] == segments[0] + 1, told[1], 0)
    index = jnp.arange(tokens, dtype=jnp.int32)
    positions = jnp.where(index < rise, index + ahead, index - rise)
    spot = jnp.stack([rise, ahead]).astype(jnp.int32)
    cosine, sine = rotary_tables(positions)

    query, kv, query_raw, key_raw, weight = qkv_call(
        tab, hidden_in, gains, heads, qkv_packed, cosine, sine
    )
    kv_prev = shifted(kv[tokens - WINDOW :], 1)
    held_out = spread(held_out, over_plane, query)
    *upper, out = attend_call(
        tokens - 2 * TILE, spot, tab, query, kv, (held_out, swapped(held_out, 1)), ()
    )
    kv_low = jnp.concatenate([after(kv_prev, *upper), kv[: tokens - WINDOW]])
    attended, attn_out, stat = attend_call(0, spot, tab, query, kv_low, (out,), upper)

    routes = ((2, 4, 8, 16), (4, 8, 2, 16), (8, 2, 4, 16))
    tabs = [chip_table(me, route[::-1]) for route in routes]
    output, d_mid, d_attn, d_gains, *pieces = ffn_call(
        tabs, hidden_in, attn_out, cotangent, gains, ffn_packed
    )
    came = [swapped(pieces[2 * i + 1], 1) for i in range(3)]
    keep_out, send_out = out_call(tabs[2], d_attn, attended)
    came.append(swapped(send_out, 1))
    d_query, d_head0, dkv_low = attend_back_call(
        0, spot, query, kv_low, after(d_attn, send_out), out, stat, query_raw, cosine, sine, heads, ()
    )
    came = [after(one, dkv_low) for one in came]
    held = [(pieces[0], came[0]), (pieces[2], came[1])]
    held.append((jnp.concatenate([pieces[4], keep_out], axis=1), jnp.concatenate(came[2:], axis=1)))
    halo = shifted(dkv_low[:WINDOW].astype(bf16), -1)
    halves = halved(held, routes, 0)
    d_query, d_head1, dkv_high = attend_back_call(
        tokens - 2 * TILE, spot, query, kv, after(d_attn, *[one[1] for one in halves]), out, stat,
        query_raw, cosine, sine, heads, (d_query,),
    )
    held = sent(halves, dkv_high)
    halves = halved(held, routes, 1)
    d_qkv, keep_qkv, send_qkv = qkv_grad_call(
        tab, after(hidden_in, *[one[1] for one in halves]), gains, heads, d_query, dkv_high, dkv_low, halo,
        key_raw, cosine, sine, weight, d_gains, d_head0, d_head1,
    )
    held = sent(halves, keep_qkv)
    halves = halved(held, routes, 2)
    grad_in = input_grad_call(
        after(hidden_in, *[one[1] for one in halves]), gains, after(d_qkv, send_qkv), weight, d_mid
    )
    total = keep_qkv.astype(f32) + after(swapped(send_qkv, 1), grad_in).astype(f32)
    held = sent(halves, grad_in)
    halves = halved(held, routes, 3)
    total = after(total, *[one[1] for one in halves])
    total = collected(total, over_plane)
    sum_gate, sum_up, sum_down = settled(sent(halves))
    sum_qkv = collected(total, over_z)[0]
    sum_down, sum_out = sum_down[:64], sum_down[64:]

    gate_up = [one.reshape(-1, ROWS, LANES).transpose(1, 0, 2).reshape(-1) for one in (sum_gate, sum_up)]
    parts = sum_qkv[: 4 * ROWS].reshape(4, ROWS, GROUP).transpose(1, 0, 2).reshape(ROWS, QKV)
    summed = (
        parts[:, : NH * HD].reshape(-1),
        parts[:, NH * HD : NH * HD + HD].reshape(-1),
        parts[:, NH * HD + HD :].reshape(-1),
        sum_out.reshape(-1),
        gate_up[0],
        gate_up[1],
        sum_down.reshape(-1),
        sum_qkv[4 * ROWS, : s_gain.shape[0]],
    )
    if near > 1:
        summed = tuple(
            lax.psum_scatter(one, "flat", scatter_dimension=0, tiled=True, axis_index_groups=groups)
            for one in summed
        )
    return (output, grad_in) + tuple(summed)


def solution(mesh):
    rows = P("flat", None)
    flat = P("flat")
    return jax.shard_map(
        per_device,
        mesh=mesh,
        in_specs=(rows,) + (flat,) * 9 + (rows,),
        out_specs=(rows, rows) + (flat,) * 8,
        check_vma=False,
    )
```
